128 devices in a mesh: gx: 16 (over z_lo, y, core), gy: 8 (over x, z_hi).
Axes of the slice: x: 4, y: 4, z: 4 (z_hi: 2, z_lo: 2; z = z_hi * 2 + z_lo), core: 2. Of those that a mesh axis runs over, the one named last changes fastest.
Arguments:
- density: float32 [256, 1024, 256], P('gx', 'gy'), may hold values from 0.5 to 5
- cotangent: float32 [3, 256, 1024, 256], P(None, 'gx', 'gy'), may hold values from -60 to 60
- features: bfloat16 [8, 256, 1024, 256], P(None, 'gx', 'gy'), may hold values from -6 to 6
- w_inner: bfloat16 [64, 8], replicated, may hold values from -2 to 2
- w_outer: bfloat16 [3, 64], replicated, may hold values from -0.75 to 0.75
Outputs:
- grad_velocity: float32 [3, 256, 1024, 256], P(None, 'gx', 'gy')
- grad_inner: float32 [64, 8], replicated
- grad_outer: float32 [3, 64], replicated
The draws below stay inside these ranges and needn't reach their ends.
All inputs are finite; a program needn't handle non-finite values.
Results may differ from the reference program's by a relative error of at most 0.0003.
Values sent between devices are 32-bit elements; how exact they have to be, the bound alone decides.
No kernel may reach another device: no remote copies, remote signals or barrier semaphores. Data moves between devices by JAX's collectives and lax.ppermute only.
A program may use at most 128 MiB of HBM per device.

```python
import math
import jax
import jax.numpy as jnp
from jax import lax

F = 8
H = 64
ITERS = 2
NX = 256
NY = 1024
NZ = 256


def shared_part(key):
    return jax.random.truncated_normal(key, -4.0, 4.0, (3, NX, NY, NZ), jnp.float32)


def draw_features(key, part):
    common = shared_part(key)
    key = jax.random.fold_in(key, 11)
    own = jax.random.truncated_normal(key, -4.0, 4.0, (F, NX, NY, NZ), jnp.float32)
    head = 0.7 * common + 0.7 * own[:3]
    return jnp.concatenate([head, own[3:]], 0).astype(jnp.bfloat16)


def draw_cotangent(key, part):
    common = shared_part(key)
    key = jax.random.fold_in(key, 12)
    first, second = jax.random.split(key)
    position = jnp.arange(NX, dtype=jnp.float32) / max(NX - 1, 1)
    ramp = jnp.exp(math.log(3.0) * position).reshape(1, NX, 1, 1)
    rough = jnp.exp(jax.random.uniform(second, (3, NX, NY, NZ), jnp.float32, 0.0, math.log(10.0)))
    own = jax.random.truncated_normal(first, -4.0, 4.0, (3, NX, NY, NZ), jnp.float32)
    values = 0.6 * common + 0.8 * own
    return (values * ramp * rough / 3.0).astype(jnp.float32)


def steps_of(key, shape, pieces, smallest, largest):
    loudness, own = 1.0, jax.random.fold_in(key, 6)
    for dim, parts in pieces:
        draws = jnp.exp(jax.random.uniform(jax.random.fold_in(own, dim), (parts,), jnp.float32, smallest / len(pieces), largest / len(pieces)))
        loudness = loudness * jnp.repeat(draws, shape[dim] // parts).reshape([-1 if axis == dim else 1 for axis in range(len(shape))])
    return loudness


def scatter_about(own_key, dims, spread, most, kind=jnp.bfloat16):
    result = jax.random.normal(own_key, dims, jnp.float32) * spread
    return jnp.minimum(jnp.maximum(result, -most), most).astype(kind)


def setup_inputs(seed: int = 0) -> dict:
    arg_keys = jax.random.split(jax.random.key(seed), 6)
    density = jnp.clip(jnp.exp(math.log(5.0) - 2.3025851 * jax.random.uniform(arg_keys[0], (NX, NY, NZ), jnp.float32) ** steps_of(arg_keys[0], (NX, NY, NZ), ((0, 16), (1, 8)), -0.2, 0.2)), 0.5, 5.0)
    cotangent = draw_cotangent(jax.random.fold_in(arg_keys[5], 71), 0)
    features = draw_features(jax.random.fold_in(arg_keys[5], 71), 0)
    w_inner = scatter_about(arg_keys[3], (H, F), F ** -0.5, 2.0)
    w_outer = scatter_about(arg_keys[4], (3, H), H ** -0.5, 0.75)
    return {"density": density, "cotangent": cotangent, "features": features, "w_inner": w_inner, "w_outer": w_outer}


def next_cells(field, axis):
    size = field.shape[axis]
    tail = jnp.zeros_like(lax.slice_in_dim(field, 0, 1, axis=axis))
    return jnp.concatenate([lax.slice_in_dim(field, 1, size, axis=axis), tail], axis)


def prior_cells(field, axis):
    size = field.shape[axis]
    head = jnp.zeros_like(lax.slice_in_dim(field, 0, 1, axis=axis))
    return jnp.concatenate([head, lax.slice_in_dim(field, 0, size - 1, axis=axis)], axis)


def operate(field, betas):
    total = jnp.zeros_like(field)
    for axis in range(3):
        flux = betas[axis] * (next_cells(field, axis) - field)
        total = total + prior_cells(flux, axis) - flux
    return total


def closure_grads(features, gout, w_inner, w_outer):
    feats = features.reshape(features.shape[0], -1)
    gflat = gout.astype(jnp.bfloat16).reshape(3, -1)
    cells = feats.shape[1]
    width = min(cells, 65536)

    def step(index, carry):
        acc_inner, acc_outer = carry
        start = index * width
        block = lax.dynamic_slice_in_dim(feats, start, width, 1)
        gblock = lax.dynamic_slice_in_dim(gflat, start, width, 1)
        hidden = jnp.tanh(jnp.dot(w_inner, block, preferred_element_type=jnp.float32))
        hidden_b = hidden.astype(jnp.bfloat16)
        acc_outer = acc_outer + lax.dot_general(gblock, hidden_b, (((1,), (1,)), ((), ())), preferred_element_type=jnp.float32)
        back = lax.dot_general(w_outer, gblock, (((0,), (0,)), ((), ())), preferred_element_type=jnp.float32)
        dpre = (back * (1.0 - hidden * hidden)).astype(jnp.bfloat16)
        acc_inner = acc_inner + lax.dot_general(dpre, block, (((1,), (1,)), ((), ())), preferred_element_type=jnp.float32)
        return acc_inner, acc_outer

    init = (jnp.zeros((w_inner.shape[0], feats.shape[0]), jnp.float32), jnp.zeros((3, w_inner.shape[0]), jnp.float32))
    return lax.fori_loop(0, cells // width, step, init)


def reference(density, cotangent, features, w_inner, w_outer):
    betas = [2.0 / (density + next_cells(density, axis)) for axis in range(3)]
    source = jnp.zeros_like(density)
    for axis in range(3):
        weighted = betas[axis] * cotangent[axis]
        source = source + prior_cells(weighted, axis) - weighted
    multiplier = jnp.zeros_like(density)
    residual = source
    direction = source
    norm_now = jnp.sum(residual * residual)
    for step in range(ITERS):
        image = operate(direction, betas)
        alpha = norm_now / jnp.sum(direction * image)
        multiplier = multiplier + alpha * direction
        residual = residual - alpha * image
        norm_next = jnp.sum(residual * residual)
        direction = residual + (norm_next / norm_now) * direction
        norm_now = norm_next
    correction = jnp.stack([next_cells(multiplier, axis) - multiplier for axis in range(3)], 0)
    grad_velocity = cotangent - correction
    acc_inner, acc_outer = closure_grads(features, grad_velocity, w_inner, w_outer)
    count = float(NX * NY * NZ)
    return grad_velocity, acc_inner / count, acc_outer / count
```

```python
import jax
import jax.numpy as jnp
from jax import lax
from jax.experimental import pallas as pl
from jax.experimental.pallas import tpu as pltpu
from jax.sharding import PartitionSpec as P

F32 = jnp.float32
BF16 = jnp.bfloat16
LAST = (((1,), (1,)), ((), ()))
STAGES = ((8, 16), (32, 64), (1, 2), (4,))
VMEM = 56 * 2**20


def shifted(value, axis, by):
    devices = lax.axis_size(axis)
    pairs = [(i, i + by) for i in range(devices) if 0 <= i + by < devices]
    return lax.ppermute(value, axis, pairs)


def total(value):
    devices = lax.axis_size("gx") * lax.axis_size("gy")
    for bits in STAGES:
        level = [value]
        masks = [0]
        for bit in bits:
            masks = masks + [mask ^ bit for mask in masks]
        for mask in masks[1:]:
            pairs = [(i, i ^ mask) for i in range(devices)]
            level.append(lax.ppermute(value, ("gx", "gy"), pairs))
        while len(level) > 1:
            level = [level[k] + level[k + 1] for k in range(0, len(level), 2)]
        value = level[0]
    return value


def next_row(plane, row):
    size = plane.shape[0]
    at = lax.broadcasted_iota(jnp.int32, plane.shape, 0)
    return jnp.where(at == size - 1, row, pltpu.roll(plane, size - 1, 0))


def prior_row(plane, row):
    at = lax.broadcasted_iota(jnp.int32, plane.shape, 0)
    return jnp.where(at == 0, row, pltpu.roll(plane, 1, 0))


def next_lane(plane):
    size = plane.shape[1]
    at = lax.broadcasted_iota(jnp.int32, plane.shape, 1)
    return jnp.where(at == size - 1, 0.0, pltpu.roll(plane, size - 1, 1))


def prior_lane(plane):
    at = lax.broadcasted_iota(jnp.int32, plane.shape, 1)
    return jnp.where(at == 0, 0.0, pltpu.roll(plane, 1, 1))


def fold(plane):
    return jnp.sum(plane.reshape(-1, 8, plane.shape[1]), 0)


def lanes(folded):
    row = jnp.sum(folded, 0, keepdims=True)
    return sum(row[:, k : k + 128] for k in range(0, row.shape[1], 128))


def source_kernel(
    dens, cot, below_x, above_x, below_y, above_y, s_out, x_lo, x_hi, y_lo, y_hi, carry
):
    step, planes = pl.program_id(0), dens.shape[0]
    here = dens[step]
    ahead = jnp.where(step == planes - 1, above_x[...], dens[jnp.minimum(step + 1, planes - 1)])

    @pl.when(step == 0)
    def _():
        carry[...] = 2.0 / (below_x[0] + here) * below_x[1]

    flux = 2.0 / (here + ahead) * cot[0, 0]
    out = carry[...] - flux
    carry[...] = flux
    row = pl.ds(step, 1)
    first = 2.0 / (below_y[0, row] + here[:1]) * below_y[1, row]
    flux = 2.0 / (here + next_row(here, above_y[row])) * cot[1, 0]
    out = out + prior_row(flux, first) - flux
    flux = 2.0 / (here + next_lane(here)) * cot[2, 0]
    out = out + prior_lane(flux) - flux
    s_out[0] = out
    y_lo[row] = out[:1]
    y_hi[row] = out[-1:]

    @pl.when(step == 0)
    def _():
        x_lo[...] = out

    @pl.when(step == planes - 1)
    def _():
        x_hi[...] = out


def image_kernel(
    dens, s, dens_bx, dens_ax, dens_by, dens_ay, s_bx, s_ax, s_by, s_ay,
    q_out, x_lo, x_hi, y_lo, y_hi, beta_x, beta_y, sums, flux_x, acc,
):
    step, planes = pl.program_id(0), dens.shape[0]
    here, field = dens[step], s[step]
    last = step == planes - 1
    ahead = jnp.minimum(step + 1, planes - 1)
    row = pl.ds(step, 1)

    @pl.when(step == 0)
    def _():
        below = dens_bx[...]
        flux_x[...] = jnp.where(below > 0, 2.0 / (below + here) * (field - s_bx[...]), 0.0)
        acc[...] = jnp.zeros_like(acc)

    b_x = 2.0 / (here + jnp.where(last, dens_ax[...], dens[ahead]))
    flux = b_x * (jnp.where(last, s_ax[...], s[ahead]) - field)
    out = flux_x[...] - flux
    flux_x[...] = flux
    below = dens_by[row]
    first = jnp.where(below > 0, 2.0 / (below + here[:1]) * (field[:1] - s_by[row]), 0.0)
    b_y = 2.0 / (here + next_row(here, dens_ay[row]))
    flux = b_y * (next_row(field, s_ay[row]) - field)
    out = out + (prior_row(flux, first) - flux)
    b_z = 2.0 / (here + next_lane(here))
    flux = b_z * (next_lane(field) - field)
    out = out + (prior_lane(flux) - flux)
    q_out[0] = out
    y_lo[row] = out[:1]
    y_hi[row] = out[-1:]
    beta_y[row] = b_y[-1:]
    acc[0] += fold(field * field)
    acc[1] += fold(field * out)
    acc[2] += fold(out * out)
    jump = next_row(out, out[-1:]) - out
    jump_z = next_lane(out) - out
    acc[3] += fold(b_y * jump * jump + b_z * jump_z * jump_z)

    @pl.when(step == 0)
    def _():
        x_lo[...] = out

    @pl.when(step > 0)
    def _():
        jump = out - x_hi[...]
        acc[3] += fold(beta_x[...] * jump * jump)

    x_hi[...] = out
    beta_x[...] = b_x

    @pl.when(last)
    def _():
        rows = [lanes(acc[k]) for k in range(4)]
        sums[...] = jnp.concatenate(rows + [jnp.zeros((4, 128), F32)], 0)


def edge_kernel(sums, x_hi, y_hi, beta_x, beta_y, q_ax, q_ay, out):
    jump_x = q_ax[...] - x_hi[...]
    jump_y = q_ay[...] - y_hi[...]
    edge = lanes(fold(beta_x[...] * jump_x * jump_x)) + lanes(fold(beta_y[...] * jump_y * jump_y))
    at = lax.broadcasted_iota(jnp.int32, (8, 128), 0)
    out[...] = sums[...] + jnp.where(at == 3, edge, 0.0)


def closure_kernel(
    sums, cot, s, q, s_ax, q_ax, s_ay, q_ay, feats, w_in, w_out,
    grad, grads, velocity, hid, slope, vel, prod, acc_o, acc_t,
):
    step, planes = pl.program_id(0), s.shape[0]
    rows, width = s.shape[1], s.shape[2]
    count = feats.shape[0]
    m0, m1, m2, m3 = (jnp.sum(sums[k : k + 1], 1, keepdims=True) for k in range(4))
    alpha0 = m0 / m1
    rr1 = alpha0 * alpha0 * m2 - m0
    beta = rr1 / m0
    more = 1.0 + beta
    alpha1 = rr1 / (more * more * m1 - 2.0 * more * alpha0 * m2 + alpha0 * alpha0 * m3)
    on_s, on_q = alpha0 + alpha1 * more, -alpha1 * alpha0

    @pl.when(step == 0)
    def _():
        acc_o[...] = jnp.zeros_like(acc_o)
        acc_t[...] = jnp.zeros_like(acc_t)

    last = step == planes - 1
    ahead = jnp.minimum(step + 1, planes - 1)
    row = pl.ds(step, 1)
    here = on_s * s[step] + on_q * q[step]
    beyond = on_s * jnp.where(last, s_ax[...], s[ahead]) + on_q * jnp.where(last, q_ax[...], q[ahead])
    edge = on_s * s_ay[row] + on_q * q_ay[row]
    for a, after in enumerate((beyond, next_row(here, edge), next_lane(here))):
        value = cot[a, 0] - (after - here)
        grad[a, 0] = value
        velocity[a] = value.astype(BF16).astype(F32)

    half = w_in.shape[0] // 2
    for block in range(rows // 16):
        at = slice(block * 16, block * 16 + 16)
        inner = feats[:, 0, at, :].reshape(count * 16, width)
        pre = lax.dot_general(
            w_in[...], inner, (((1,), (0,)), ((), ())), preferred_element_type=F32
        )
        hidden = jnp.tanh(pre)
        hidden_b = hidden.astype(BF16)
        slope_b = (1.0 - hidden * hidden).astype(BF16)
        wide = [feats[c, 0, at, :].astype(F32) for c in range(count)]
        for part in range(2):
            to = slice((block * 2 + part) * width, (block * 2 + part + 1) * width)
            hid[:, to] = hidden_b[part * half : (part + 1) * half]
            slope[:, to] = slope_b[part * half : (part + 1) * half]
            low = block * 16 + part * 8
            vs = [velocity[a, low : low + 8, :] for a in range(3)]
            vel[:, to] = jnp.concatenate(vs + [jnp.zeros_like(vs[0])], 0).astype(BF16)
            fs = [f[part * 8 : part * 8 + 8] for f in wide]
            prod[:, to] = jnp.concatenate([v * f for v in vs for f in fs], 0).astype(BF16)
    acc_o[...] += lax.dot_general(vel[...], hid[...], LAST, preferred_element_type=F32)
    acc_t[...] += lax.dot_general(prod[...], slope[...], LAST, preferred_element_type=F32)

    @pl.when(last)
    def _():
        def own(value):
            at_row = lax.broadcasted_iota(jnp.int32, value.shape, 0) % 8
            at_col = lax.broadcasted_iota(jnp.int32, value.shape, 1) % 8
            kept = jnp.where(at_row == at_col, value, 0.0)
            return jnp.sum(kept.reshape(-1, 8, value.shape[1]), 1)

        outer = own(acc_o[...])
        terms = own(acc_t[...])
        inner = sum(
            w_out[a : a + 1] * terms[a * count : (a + 1) * count] for a in range(3)
        )
        both = jnp.concatenate([inner, outer, jnp.zeros_like(outer)], 0)
        hidden_at = lax.broadcasted_iota(jnp.int32, (half, 128), 0) // 8
        column = lax.broadcasted_iota(jnp.int32, (half, 128), 1)
        pick = (hidden_at == column).astype(F32)
        grads[...] = jnp.dot(
            both, pick, precision=lax.Precision.HIGHEST, preferred_element_type=F32
        )


def whole(shape):
    return pl.BlockSpec(shape, lambda i: (0,) * len(shape))


def shape(*dims):
    return jax.ShapeDtypeStruct(dims, F32)


def params():
    return pltpu.CompilerParams(vmem_limit_bytes=VMEM)


def body(density, cotangent, features, w_inner, w_outer):
    nx, ny, nz = density.shape
    count, hidden = features.shape[0], w_inner.shape[0]
    cells = float(density.size * lax.axis_size("gx") * lax.axis_size("gy"))
    field, side_x, side_y = (nx, ny, nz), (ny, nz), (nx, nz)
    plane = pl.BlockSpec((1, ny, nz), lambda i: (i, 0, 0))
    planes = pl.BlockSpec((3, 1, ny, nz), lambda i: (0, i, 0, 0))

    dens_ax = shifted(density[0], "gx", -1)
    below_x = shifted(jnp.stack([density[-1], cotangent[0, -1]]), "gx", 1)
    dens_ay = shifted(density[:, 0], "gy", -1)
    below_y = shifted(jnp.stack([density[:, -1], cotangent[1, :, -1]]), "gy", 1)

    pick = jnp.arange(16)[None, None, :] == jnp.arange(16).reshape(2, 8)[:, :, None]
    w_in = w_inner[None, :, None, :, None] * pick[:, None, :, None, :].astype(BF16)
    w_in = w_in.reshape(2 * hidden * 8, count * 16)
    w_out = jnp.repeat(w_outer.astype(F32), 8, axis=1)

    s, s_x0, s_x1, s_y0, s_y1 = pl.pallas_call(
        source_kernel,
        grid=(nx,),
        in_specs=[whole(field), planes, whole((2,) + side_x), whole(side_x), whole((2,) + side_y), whole(side_y)],
        out_specs=[plane, whole(side_x), whole(side_x), whole(side_y), whole(side_y)],
        out_shape=[shape(*field), shape(*side_x), shape(*side_x), shape(*side_y), shape(*side_y)],
        scratch_shapes=[pltpu.VMEM(side_x, F32)],
        compiler_params=params(),
    )(density, cotangent, below_x, dens_ax, below_y, dens_ay)

    s_ax = shifted(s_x0, "gx", -1)
    s_bx = shifted(s_x1, "gx", 1)
    s_ay = shifted(s_y0, "gy", -1)
    s_by = shifted(s_y1, "gy", 1)

    q, q_x0, q_x1, q_y0, q_y1, beta_x, beta_y, sums = pl.pallas_call(
        image_kernel,
        grid=(nx,),
        in_specs=[whole(field)] * 2 + [whole(side_x)] * 2 + [whole(side_y)] * 2 + [whole(side_x)] * 2 + [whole(side_y)] * 2,
        out_specs=[plane, whole(side_x), whole(side_x), whole(side_y), whole(side_y), whole(side_x), whole(side_y), whole((8, 128))],
        out_shape=[shape(*field), shape(*side_x), shape(*side_x), shape(*side_y), shape(*side_y), shape(*side_x), shape(*side_y), shape(8, 128)],
        scratch_shapes=[pltpu.VMEM(side_x, F32), pltpu.VMEM((4, 8, nz), F32)],
        compiler_params=params(),
    )(density, s, below_x[0], dens_ax, below_y[0], dens_ay, s_bx, s_ax, s_by, s_ay)

    q_ax = shifted(q_x0, "gx", -1)
    q_ay = shifted(q_y0, "gy", -1)
    sums = pl.pallas_call(edge_kernel, out_shape=shape(8, 128), compiler_params=params())(
        sums, q_x1, q_y1, beta_x, beta_y, q_ax, q_ay
    )
    sums = total(sums)

    half = hidden * 8
    long = ny // 8 * nz
    grad, grads = pl.pallas_call(
        closure_kernel,
        grid=(nx,),
        in_specs=[
            whole((8, 128)), planes, whole(field), whole(field), whole(side_x), whole(side_x), whole(side_y), whole(side_y),
            pl.BlockSpec((count, 1, ny, nz), lambda i: (0, i, 0, 0)), whole(w_in.shape), whole(w_out.shape),
        ],
        out_specs=[planes, whole((16, 128))],
        out_shape=[shape(3, *field), shape(16, 128)],
        scratch_shapes=[
            pltpu.VMEM((3, ny, nz), F32),
            pltpu.VMEM((half, long), BF16),
            pltpu.VMEM((half, long), BF16),
            pltpu.VMEM((32, long), BF16),
            pltpu.VMEM((24 * count, long), BF16),
            pltpu.VMEM((32, half), F32),
            pltpu.VMEM((24 * count, half), F32),
        ],
        compiler_params=params(),
    )(sums, cotangent, s, q, s_ax, q_ax, s_ay, q_ay, features, w_in, w_out)
    grads = total(grads) / cells
    return grad, grads[:count, :hidden].T, grads[count : count + 3, :hidden]


def solution(mesh):
    in_specs = (P("gx", "gy", None), P(None, "gx", "gy", None), P(None, "gx", "gy", None), P(), P())
    out_specs = (P(None, "gx", "gy", None), P(), P())
    return jax.shard_map(body, mesh=mesh, in_specs=in_specs, out_specs=out_specs, check_vma=False)
```

```python
import jax
import jax.numpy as jnp
from jax import lax
from jax.experimental import pallas as pl
from jax.experimental.pallas import tpu as pltpu
from jax.sharding import PartitionSpec as P

F32 = jnp.float32
BF16 = jnp.bfloat16
PLAIN = (((1,), (0,)), ((), ()))
FIRST = (((0,), (0,)), ((), ()))
VMEM = 56 * 2**20


def shifted(value, axis, by):
    devices = lax.axis_size(axis)
    pairs = [(i, i + by) for i in range(devices) if 0 <= i + by < devices]
    return lax.ppermute(value, axis, pairs)


def collect(copies):
    return lax.all_to_all(copies, ("gx", "gy"), 0, 0)


def next_row(plane, row):
    size = plane.shape[0]
    at = lax.broadcasted_iota(jnp.int32, plane.shape, 0)
    return jnp.where(at == size - 1, row, pltpu.roll(plane, size - 1, 0))


def prior_row(plane, row):
    at = lax.broadcasted_iota(jnp.int32, plane.shape, 0)
    return jnp.where(at == 0, row, pltpu.roll(plane, 1, 0))


def next_lane(plane):
    size = plane.shape[1]
    at = lax.broadcasted_iota(jnp.int32, plane.shape, 1)
    return jnp.where(at == size - 1, 0.0, pltpu.roll(plane, size - 1, 1))


def prior_lane(plane):
    at = lax.broadcasted_iota(jnp.int32, plane.shape, 1)
    return jnp.where(at == 0, 0.0, pltpu.roll(plane, 1, 1))


def fold(plane):
    return jnp.sum(plane.reshape(-1, 8, plane.shape[1]), 0)


def lanes(folded):
    row = jnp.sum(folded, 0, keepdims=True)
    return sum(row[:, k : k + 128] for k in range(0, row.shape[1], 128))


def source_kernel(
    dens, cot, below_x, above_x, below_y, above_y, s_out, x_lo, x_hi, y_lo, y_hi, carry
):
    step, planes = pl.program_id(0), dens.shape[0]
    here = dens[step]
    ahead = jnp.where(step == planes - 1, above_x[...], dens[jnp.minimum(step + 1, planes - 1)])

    @pl.when(step == 0)
    def _():
        carry[...] = 2.0 / (below_x[0] + here) * below_x[1]

    flux = 2.0 / (here + ahead) * cot[0, 0]
    out = carry[...] - flux
    carry[...] = flux
    row = pl.ds(step, 1)
    first = 2.0 / (below_y[0, row] + here[:1]) * below_y[1, row]
    flux = 2.0 / (here + next_row(here, above_y[row])) * cot[1, 0]
    out = out + prior_row(flux, first) - flux
    flux = 2.0 / (here + next_lane(here)) * cot[2, 0]
    out = out + prior_lane(flux) - flux
    s_out[0] = out
    y_lo[row] = out[:1]
    y_hi[row] = out[-1:]

    @pl.when(step == 0)
    def _():
        x_lo[...] = out

    @pl.when(step == planes - 1)
    def _():
        x_hi[...] = out


def image_kernel(
    dens, s, dens_bx, dens_ax, dens_by, dens_ay, s_bx, s_ax, s_by, s_ay,
    q_out, x_lo, x_hi, y_lo, y_hi, beta_x, beta_y, sums, flux_x, acc,
):
    step, planes = pl.program_id(0), dens.shape[0]
    here, field = dens[step], s[step]
    last = step == planes - 1
    ahead = jnp.minimum(step + 1, planes - 1)
    row = pl.ds(step, 1)

    @pl.when(step == 0)
    def _():
        below = dens_bx[...]
        flux_x[...] = jnp.where(below > 0, 2.0 / (below + here) * (field - s_bx[...]), 0.0)
        acc[...] = jnp.zeros_like(acc)

    b_x = 2.0 / (here + jnp.where(last, dens_ax[...], dens[ahead]))
    flux = b_x * (jnp.where(last, s_ax[...], s[ahead]) - field)
    out = flux_x[...] - flux
    flux_x[...] = flux
    below = dens_by[row]
    first = jnp.where(below > 0, 2.0 / (below + here[:1]) * (field[:1] - s_by[row]), 0.0)
    b_y = 2.0 / (here + next_row(here, dens_ay[row]))
    flux = b_y * (next_row(field, s_ay[row]) - field)
    out = out + (prior_row(flux, first) - flux)
    b_z = 2.0 / (here + next_lane(here))
    flux = b_z * (next_lane(field) - field)
    out = out + (prior_lane(flux) - flux)
    q_out[0] = out
    y_lo[row] = out[:1]
    y_hi[row] = out[-1:]
    beta_y[row] = b_y[-1:]
    acc[0] += fold(field * field)
    acc[1] += fold(field * out)
    acc[2] += fold(out * out)
    jump = next_row(out, out[-1:]) - out
    jump_z = next_lane(out) - out
    acc[3] += fold(b_y * jump * jump + b_z * jump_z * jump_z)

    @pl.when(step == 0)
    def _():
        x_lo[...] = out

    @pl.when(step > 0)
    def _():
        jump = out - x_hi[...]
        acc[3] += fold(beta_x[...] * jump * jump)

    x_hi[...] = out
    beta_x[...] = b_x

    @pl.when(last)
    def _():
        rows = [lanes(acc[k]) for k in range(4)]
        sums[...] = jnp.concatenate(rows + [jnp.zeros((4, 128), F32)], 0)


def edge_kernel(sums, x_hi, y_hi, beta_x, beta_y, q_ax, q_ay, out):
    jump_x = q_ax[...] - x_hi[...]
    jump_y = q_ay[...] - y_hi[...]
    edge = lanes(fold(beta_x[...] * jump_x * jump_x)) + lanes(fold(beta_y[...] * jump_y * jump_y))
    at = lax.broadcasted_iota(jnp.int32, (8, 128), 0)
    each = jnp.sum(sums[...] + jnp.where(at == 3, edge, 0.0), 1, keepdims=True)
    at_lane = lax.broadcasted_iota(jnp.int32, (8, 128), 1)
    row = jnp.sum(jnp.where(at == at_lane, each, 0.0), 0, keepdims=True)
    out[...] = jnp.broadcast_to(row, out.shape)


def closure_kernel(
    sums, cot, s, q, s_ax, q_ax, s_ay, q_ay, feats, w_in, w_out,
    grad, grads, scale, velocity, hid, slope, vel, prod, acc_o, acc_t,
):
    step, planes = pl.program_id(0), s.shape[0]
    rows, width = s.shape[1], s.shape[2]
    count = feats.shape[0]

    @pl.when(step == 0)
    def _():
        all_sums = jnp.sum(sums[...], 0, keepdims=True)
        at_lane = lax.broadcasted_iota(jnp.int32, (1, 128), 1)
        m0, m1, m2, m3 = (
            jnp.sum(jnp.where(at_lane == k, all_sums, 0.0), 1, keepdims=True) for k in range(4)
        )
        alpha0 = m0 / m1
        rr1 = alpha0 * alpha0 * m2 - m0
        beta = rr1 / m0
        more = 1.0 + beta
        alpha1 = rr1 / (more * more * m1 - 2.0 * more * alpha0 * m2 + alpha0 * alpha0 * m3)
        scale[0] = jnp.broadcast_to(alpha0 + alpha1 * more, scale.shape[1:])
        scale[1] = jnp.broadcast_to(-alpha1 * alpha0, scale.shape[1:])
        acc_o[...] = jnp.zeros_like(acc_o)
        acc_t[...] = jnp.zeros_like(acc_t)

    on_s, on_q = scale[0][:1], scale[1][:1]
    last = step == planes - 1
    ahead = jnp.minimum(step + 1, planes - 1)
    row = pl.ds(step, 1)
    here = on_s * s[step] + on_q * q[step]
    beyond = on_s * jnp.where(last, s_ax[...], s[ahead]) + on_q * jnp.where(last, q_ax[...], q[ahead])
    edge = on_s * s_ay[row] + on_q * q_ay[row]
    for a, after in enumerate((beyond, next_row(here, edge), next_lane(here))):
        value = cot[a, 0] - (after - here)
        grad[a, 0] = value
        velocity[a] = value.astype(BF16).astype(F32)

    half = w_in.shape[1] // 2
    for block in range(rows // 16):
        at = slice(block * 16, block * 16 + 16)
        inner = feats[:, 0, at, :].reshape(count * 16, width)
        pre = lax.dot_general(inner, w_in[...], FIRST, preferred_element_type=F32)
        hidden = jnp.tanh(pre)
        hidden_b = hidden.astype(BF16)
        slope_b = (1.0 - hidden * hidden).astype(BF16)
        wide = [feats[c, 0, at, :].astype(F32) for c in range(count)]
        for part in range(2):
            to = slice((block * 2 + part) * width, (block * 2 + part + 1) * width)
            hid[to, :] = hidden_b[:, part * half : (part + 1) * half]
            slope[to, :] = slope_b[:, part * half : (part + 1) * half]
            low = block * 16 + part * 8
            vs = [velocity[a, low : low + 8, :] for a in range(3)]
            vel[:, to] = jnp.concatenate(vs + [jnp.zeros_like(vs[0])], 0).astype(BF16)
            fs = [f[part * 8 : part * 8 + 8] for f in wide]
            prod[:, to] = jnp.concatenate([v * f for v in vs for f in fs], 0).astype(BF16)
    acc_o[...] += lax.dot_general(vel[...], hid[...], PLAIN, preferred_element_type=F32)
    acc_t[...] += lax.dot_general(prod[...], slope[...], PLAIN, preferred_element_type=F32)

    @pl.when(last)
    def _():
        def own(value):
            at_row = lax.broadcasted_iota(jnp.int32, value.shape, 0) % 8
            at_col = lax.broadcasted_iota(jnp.int32, value.shape, 1) % 8
            kept = jnp.where(at_row == at_col, value, 0.0)
            return jnp.sum(kept.reshape(-1, 8, value.shape[1]), 1)

        outer = own(acc_o[...])
        terms = own(acc_t[...])
        inner = sum(
            w_out[a : a + 1] * terms[a * count : (a + 1) * count] for a in range(3)
        )
        both = jnp.concatenate([inner, outer[:3], jnp.zeros((5, half), F32)], 0)
        hidden_at = lax.broadcasted_iota(jnp.int32, (half, 64), 0) // 8
        column = lax.broadcasted_iota(jnp.int32, (half, 64), 1)
        pick = (hidden_at == column).astype(F32)
        sums16 = jnp.dot(both, pick, precision=lax.Precision.HIGHEST, preferred_element_type=F32)
        value = jnp.concatenate([sums16[:8], sums16[8:]], 1)
        grads[...] = jnp.broadcast_to(value[None], grads.shape)


def whole(shape):
    return pl.BlockSpec(shape, lambda i: (0,) * len(shape))


def shape(*dims):
    return jax.ShapeDtypeStruct(dims, F32)


def params():
    return pltpu.CompilerParams(vmem_limit_bytes=VMEM)


def body(density, cotangent, features, w_inner, w_outer):
    nx, ny, nz = density.shape
    count, hidden = features.shape[0], w_inner.shape[0]
    devices = lax.axis_size("gx") * lax.axis_size("gy")
    cells = float(density.size * devices)
    field, side_x, side_y = (nx, ny, nz), (ny, nz), (nx, nz)
    plane = pl.BlockSpec((1, ny, nz), lambda i: (i, 0, 0))
    planes = pl.BlockSpec((3, 1, ny, nz), lambda i: (0, i, 0, 0))

    dens_ax = shifted(density[0], "gx", -1)
    below_x = shifted(jnp.stack([density[-1], cotangent[0, -1]]), "gx", 1)
    dens_ay = shifted(density[:, 0], "gy", -1)
    below_y = shifted(jnp.stack([density[:, -1], cotangent[1, :, -1]]), "gy", 1)

    pick = jnp.arange(16)[:, None, None] == jnp.arange(16).reshape(1, 2, 8)
    w_in = w_inner.T[:, None, None, :, None] * pick[None, :, :, None, :].astype(BF16)
    w_in = w_in.reshape(count * 16, 2 * hidden * 8)
    w_out = jnp.repeat(w_outer.astype(F32), 8, axis=1)

    s, s_x0, s_x1, s_y0, s_y1 = pl.pallas_call(
        source_kernel,
        grid=(nx,),
        in_specs=[whole(field), planes, whole((2,) + side_x), whole(side_x), whole((2,) + side_y), whole(side_y)],
        out_specs=[plane, whole(side_x), whole(side_x), whole(side_y), whole(side_y)],
        out_shape=[shape(*field), shape(*side_x), shape(*side_x), shape(*side_y), shape(*side_y)],
        scratch_shapes=[pltpu.VMEM(side_x, F32)],
        compiler_params=params(),
    )(density, cotangent, below_x, dens_ax, below_y, dens_ay)

    s_ax = shifted(s_x0, "gx", -1)
    s_bx = shifted(s_x1, "gx", 1)
    s_ay = shifted(s_y0, "gy", -1)
    s_by = shifted(s_y1, "gy", 1)

    q, q_x0, q_x1, q_y0, q_y1, beta_x, beta_y, sums = pl.pallas_call(
        image_kernel,
        grid=(nx,),
        in_specs=[whole(field)] * 2 + [whole(side_x)] * 2 + [whole(side_y)] * 2 + [whole(side_x)] * 2 + [whole(side_y)] * 2,
        out_specs=[plane, whole(side_x), whole(side_x), whole(side_y), whole(side_y), whole(side_x), whole(side_y), whole((8, 128))],
        out_shape=[shape(*field), shape(*side_x), shape(*side_x), shape(*side_y), shape(*side_y), shape(*side_x), shape(*side_y), shape(8, 128)],
        scratch_shapes=[pltpu.VMEM(side_x, F32), pltpu.VMEM((4, 8, nz), F32)],
        compiler_params=params(),
    )(density, s, below_x[0], dens_ax, below_y[0], dens_ay, s_bx, s_ax, s_by, s_ay)

    q_ax = shifted(q_x0, "gx", -1)
    q_ay = shifted(q_y0, "gy", -1)
    sums = pl.pallas_call(edge_kernel, out_shape=shape(devices, 128), compiler_params=params())(
        sums, q_x1, q_y1, beta_x, beta_y, q_ax, q_ay
    )
    sums = collect(sums)

    half = hidden * 8
    long = ny // 8 * nz
    grad, grads = pl.pallas_call(
        closure_kernel,
        grid=(nx,),
        in_specs=[
            whole((devices, 128)), planes, whole(field), whole(field), whole(side_x), whole(side_x), whole(side_y), whole(side_y),
            pl.BlockSpec((count, 1, ny, nz), lambda i: (0, i, 0, 0)), whole(w_in.shape), whole(w_out.shape),
        ],
        out_specs=[planes, whole((devices, 8, 128))],
        out_shape=[shape(3, *field), shape(devices, 8, 128)],
        scratch_shapes=[
            pltpu.VMEM((2, 8, nz), F32),
            pltpu.VMEM((3, ny, nz), F32),
            pltpu.VMEM((long, half), BF16),
            pltpu.VMEM((long, half), BF16),
            pltpu.VMEM((32, long), BF16),
            pltpu.VMEM((24 * count, long), BF16),
            pltpu.VMEM((32, half), F32),
            pltpu.VMEM((24 * count, half), F32),
        ],
        compiler_params=params(),
    )(sums, cotangent, s, q, s_ax, q_ax, s_ay, q_ay, features, w_in, w_out)
    grads = jnp.sum(collect(grads), 0) / cells
    return grad, grads[:, :hidden].T, grads[:3, hidden:]


def solution(mesh):
    in_specs = (P("gx", "gy", None), P(None, "gx", "gy", None), P(None, "gx", "gy", None), P(), P())
    out_specs = (P(None, "gx", "gy", None), P(), P())
    return jax.shard_map(body, mesh=mesh, in_specs=in_specs, out_specs=out_specs, check_vma=False)
```

```python
import jax
import jax.numpy as jnp
from jax import lax
from jax.experimental import pallas as pl
from jax.experimental.pallas import tpu as pltpu
from jax.sharding import PartitionSpec as P

F32 = jnp.float32
BF16 = jnp.bfloat16
PLAIN = (((1,), (0,)), ((), ()))
FIRST = (((0,), (0,)), ((), ()))
VMEM = 56 * 2**20


def collect(copies):
    return lax.all_to_all(copies, ("gx", "gy"), 0, 0)


def neighbours(value, by_x, by_y):
    nx, ny = lax.axis_size("gx"), lax.axis_size("gy")
    pairs = [
        (i * ny + j, (i + by_x) * ny + j + by_y)
        for i in range(nx)
        for j in range(ny)
        if 0 <= i + by_x < nx and 0 <= j + by_y < ny
    ]
    return lax.ppermute(value, ("gx", "gy"), pairs)


def next_lane(plane):
    size = plane.shape[1]
    at = lax.broadcasted_iota(jnp.int32, plane.shape, 1)
    return jnp.where(at == size - 1, 0.0, pltpu.roll(plane, size - 1, 1))


def prior_lane(plane):
    at = lax.broadcasted_iota(jnp.int32, plane.shape, 1)
    return jnp.where(at == 0, 0.0, pltpu.roll(plane, 1, 1))


def next_row(plane):
    return pltpu.roll(plane, plane.shape[0] - 1, 0)


def prior_row(plane):
    return pltpu.roll(plane, 1, 0)


def fold(plane):
    return jnp.sum(plane.reshape(-1, 8, plane.shape[1]), 0)


def twice_over(value):
    return 2.0 / value


LOWER_X = ((0, 2), (1, 2), (2, 1), (3, 1))
UPPER_X = ((0, 3), (1, 2), (2, 2), (3, 2))
LOWER_Y = ((0, 2), (1, 1), (2, 2), (3, 1))
UPPER_Y = ((0, 3), (1, 2), (2, 2), (3, 2))


def starts(plan):
    places, at = [], 0
    for _, width in plan:
        places.append(at)
        at += width
    return places, at


def pack_kernel(
    d_first, d_last, c_first, c_last, d_low, d_high, c_low, c_high,
    up_x, down_x, up_y, down_y, up_up, up_down, down_up, down_down,
):
    planes = d_first.shape[0]
    for plan, to, d, c, low in ((LOWER_X, up_x, d_high, c_high, False), (UPPER_X, down_x, d_low, c_low, True)):
        at = 0
        for field, width in plan:
            block = d if field == 0 else c.at[field - 1]
            first = 0 if low else block.shape[0] - width
            for x in range(first, first + width):
                to[at] = block[x]
                at += 1

    def line(field, x, y):
        if field == 0:
            block = d_first if y >= 0 else d_last
            return block[x, y % 8 : y % 8 + 1, :]
        block = c_first if y >= 0 else c_last
        return block[field - 1, x, y % 8 : y % 8 + 1, :]

    for plan, to, low in ((LOWER_Y, up_y, False), (UPPER_Y, down_y, True)):
        at = 0
        for field, width in plan:
            for y in range(width):
                for x in range(planes):
                    to[at : at + 1, :] = line(field, x, y if low else y - width)
                    at += 1
    for to, first_x, first_y in (
        (up_up, planes - 2, -2), (up_down, planes - 2, 0), (down_up, 0, -2), (down_down, 0, 0),
    ):
        at = 0
        for field in range(4):
            for x in (first_x, first_x + 1):
                for y in (first_y, first_y + 1):
                    to[at : at + 1, :] = line(field, x, y)
                    at += 1


def moments_kernel(
    dens, cot, below_x, above_x, below_y, above_y, low_low, low_high, high_low, high_high,
    s_out, q_out, sums, d_all, b_x, b_y, b_z, s_all, before, acc,
):
    planes, rows, width = dens.shape
    own = slice(8, rows + 8)
    lower_x, upper_x = starts(LOWER_X)[0], starts(UPPER_X)[0]
    lower_y, upper_y = starts(LOWER_Y)[0], starts(UPPER_Y)[0]

    def tiles(below, above):
        low, high = (8 - sum(part.shape[0] for part in parts) for parts in (below, above))
        low = jnp.concatenate([jnp.zeros((low, width), F32)] + below, 0)
        return low, jnp.concatenate(above + [jnp.zeros((high, width), F32)], 0)

    def sides(field, x):
        low, high = LOWER_Y[field][1], UPPER_Y[field][1]
        below = [below_y[pl.ds((lower_y[field] + k) * planes + x, 1), :] for k in range(low)]
        above = [above_y[pl.ds((upper_y[field] + k) * planes + x, 1), :] for k in range(high)]
        return tiles(below, above)

    def corners(field, x):
        low, high = (low_low, low_high) if x < 0 else (high_low, high_high)
        at = field * 4 + (x % 2) * 2
        return tiles([low[at : at + 2, :]], [high[at : at + 2, :]])

    def plane_of(field, x):
        if x < 0:
            return below_x[lower_x[field] + x + LOWER_X[field][1]]
        return above_x[upper_x[field] + x - planes]

    def put(x, low, middle, high):
        d_all[x + 2, 0:8, :] = low
        d_all[x + 2, own, :] = middle
        d_all[x + 2, rows + 8 : rows + 16, :] = high

    def fill(x, carry):
        low, high = sides(0, x)
        put(x, low, dens[x], high)
        return carry

    for x in (-2, -1, planes, planes + 1):
        low, high = corners(0, x)
        put(x, low, plane_of(0, x), high)
    none = jnp.zeros((8, width), F32)
    put(planes + 2, none, plane_of(0, planes + 2), none)
    lax.fori_loop(0, planes, fill, 0)

    def weight(value, inside, after):
        return jnp.where(inside, twice_over(value + after), 0.0)

    def outer_field(field, x):
        low, high = corners(field, x)
        return jnp.concatenate([low, plane_of(field, x), high], 0)

    def own_field(field, x):
        low, high = sides(field, x)
        return jnp.concatenate([low, cot[field - 1, x], high], 0)

    def source(x, field_of):
        at = x + 2
        here = d_all[at]
        inside = here > 0
        beta = weight(here, inside, d_all[at + 1])
        b_x[at] = beta
        flux = beta * field_of(1, x)
        out = before[...] - flux
        before[...] = flux
        beta = weight(here, inside, next_row(here))
        b_y[at] = beta
        flux = beta * field_of(2, x)
        out = out + prior_row(flux) - flux
        beta = weight(here, inside, next_lane(here))
        b_z[at] = beta
        flux = beta * field_of(3, x)
        out = out + prior_lane(flux) - flux
        s_all[at] = jnp.where(inside, out, 0.0)

    here = d_all[0]
    before[...] = weight(here, here > 0, d_all[1]) * outer_field(1, -2)
    source(-1, outer_field)

    def own_source(x, carry):
        source(x, own_field)
        return carry

    lax.fori_loop(0, planes, own_source, 0)
    source(planes, outer_field)
    source(planes + 1, outer_field)

    def image(x):
        at = x + 2
        here = s_all[at]
        flux = b_x[at] * (s_all[at + 1] - here)
        out = before[...] - flux
        before[...] = flux
        flux = b_y[at] * (next_row(here) - here)
        out = out + (prior_row(flux) - flux)
        flux = b_z[at] * (next_lane(here) - here)
        out = out + (prior_lane(flux) - flux)
        out = jnp.where(d_all[at] > 0, out, 0.0)
        s_out[x] = here[8:]
        q_out[x] = out[8:]
        return here, out

    def squares(x, out):
        at = x + 2
        jump = (next_row(out) - out)[own]
        jump_z = next_lane(out[own]) - out[own]
        acc[3] += fold(b_y[at, own, :] * jump * jump + b_z[at, own, :] * jump_z * jump_z)

    def jumps(x, out):
        jump = out[own] - q_out[x - 1, 0:rows, :]
        acc[3] += fold(b_x[x + 1, own, :] * jump * jump)

    def products(here, out):
        here, out = here[own], out[own]
        acc[0] += fold(here * here)
        acc[1] += fold(here * out)
        acc[2] += fold(out * out)

    before[...] = b_x[1] * (s_all[2] - s_all[1])
    acc[...] = jnp.zeros_like(acc)
    here, out = image(0)
    products(here, out)
    squares(0, out)

    def own_image(x, carry):
        here, out = image(x)
        products(here, out)
        squares(x, out)
        jumps(x, out)
        return carry

    lax.fori_loop(1, planes, own_image, 0)
    here, out = image(planes)
    jumps(planes, out)
    at = lax.broadcasted_iota(jnp.int32, (1, 128), 1)
    row = jnp.zeros((1, 128), F32)
    for k in range(4):
        value = jnp.sum(jnp.sum(acc[k], 0, keepdims=True), 1, keepdims=True)
        row = row + jnp.where(at == k, value, 0.0)
    sums[...] = jnp.broadcast_to(row, sums.shape)


def closure_kernel(
    sums, cot, s, q, feats, w_in, w_out,
    grad, grads, scale, velocity, hid, slope, vel, prod, acc_o, acc_t,
):
    step, planes = pl.program_id(0), s.shape[0] - 1
    rows, width = cot.shape[2], s.shape[2]
    count = feats.shape[0]

    @pl.when(step == 0)
    def _():
        all_sums = jnp.sum(sums[...], 0, keepdims=True)
        at_lane = lax.broadcasted_iota(jnp.int32, (1, 128), 1)
        m0, m1, m2, m3 = (
            jnp.sum(jnp.where(at_lane == k, all_sums, 0.0), 1, keepdims=True) for k in range(4)
        )
        alpha0 = m0 / m1
        rr1 = alpha0 * alpha0 * m2 - m0
        beta = rr1 / m0
        more = 1.0 + beta
        alpha1 = rr1 / (more * more * m1 - 2.0 * more * alpha0 * m2 + alpha0 * alpha0 * m3)
        scale[0] = jnp.broadcast_to(alpha0 + alpha1 * more, scale.shape[1:])
        scale[1] = jnp.broadcast_to(-alpha1 * alpha0, scale.shape[1:])
        acc_o[...] = jnp.zeros_like(acc_o)
        acc_t[...] = jnp.zeros_like(acc_t)

    on_s, on_q = scale[0][:1], scale[1][:1]
    last = step == planes - 1
    wide = on_s * s[step] + on_q * q[step]
    here = wide[:rows]
    beyond = on_s * s[step + 1, :rows, :] + on_q * q[step + 1, :rows, :]
    for a, after in enumerate((beyond, next_row(wide)[:rows], next_lane(here))):
        value = cot[a, 0] - (after - here)
        grad[a, 0] = value
        velocity[a] = value.astype(BF16).astype(F32)

    half = w_in.shape[1] // 2
    for block in range(rows // 16):
        at = slice(block * 16, block * 16 + 16)
        inner = feats[:, 0, at, :].reshape(count * 16, width)
        pre = lax.dot_general(inner, w_in[...], FIRST, preferred_element_type=F32)
        hidden = jnp.tanh(pre)
        hidden_b = hidden.astype(BF16)
        slope_b = (1.0 - hidden * hidden).astype(BF16)
        wide = [feats[c, 0, at, :].astype(F32) for c in range(count)]
        for part in range(2):
            to = slice((block * 2 + part) * width, (block * 2 + part + 1) * width)
            hid[to, :] = hidden_b[:, part * half : (part + 1) * half]
            slope[to, :] = slope_b[:, part * half : (part + 1) * half]
            low = block * 16 + part * 8
            vs = [velocity[a, low : low + 8, :] for a in range(3)]
            vel[:, to] = jnp.concatenate(vs + [jnp.zeros_like(vs[0])], 0).astype(BF16)
            fs = [f[part * 8 : part * 8 + 8] for f in wide]
            prod[:, to] = jnp.concatenate([v * f for v in vs for f in fs], 0).astype(BF16)
    acc_o[...] += lax.dot_general(vel[...], hid[...], PLAIN, preferred_element_type=F32)
    acc_t[...] += lax.dot_general(prod[...], slope[...], PLAIN, preferred_element_type=F32)

    @pl.when(last)
    def _():
        def own(value):
            at_row = lax.broadcasted_iota(jnp.int32, value.shape, 0) % 8
            at_col = lax.broadcasted_iota(jnp.int32, value.shape, 1) % 8
            kept = jnp.where(at_row == at_col, value, 0.0)
            return jnp.sum(kept.reshape(-1, 8, value.shape[1]), 1)

        outer = own(acc_o[...])
        terms = own(acc_t[...])
        inner = sum(
            w_out[a : a + 1] * terms[a * count : (a + 1) * count] for a in range(3)
        )
        both = jnp.concatenate([inner, outer[:3], jnp.zeros((5, half), F32)], 0)
        hidden_at = lax.broadcasted_iota(jnp.int32, (half, 64), 0) // 8
        column = lax.broadcasted_iota(jnp.int32, (half, 64), 1)
        pick = (hidden_at == column).astype(F32)
        sums16 = jnp.dot(both, pick, precision=lax.Precision.HIGHEST, preferred_element_type=F32)
        value = jnp.concatenate([sums16[:8], sums16[8:]], 1)
        grads[...] = jnp.broadcast_to(value[None], grads.shape)


def whole(shape):
    return pl.BlockSpec(shape, lambda i: (0,) * len(shape))


def shape(*dims):
    return jax.ShapeDtypeStruct(dims, F32)


def params():
    return pltpu.CompilerParams(vmem_limit_bytes=VMEM)


def body(density, cotangent, features, w_inner, w_outer):
    nx, ny, nz = density.shape
    count, hidden = features.shape[0], w_inner.shape[0]
    devices = lax.axis_size("gx") * lax.axis_size("gy")
    cells = float(density.size * devices)
    planes = pl.BlockSpec((3, 1, ny, nz), lambda i: (0, i, 0, 0))
    sides = [(starts(LOWER_X)[1], ny, nz), (starts(UPPER_X)[1], ny, nz), (starts(LOWER_Y)[1] * nx, nz), (starts(UPPER_Y)[1] * nx, nz)]
    corner = (16, nz)
    lines, ends = ny // 8 - 1, nx // 2 - 1
    sent = pl.pallas_call(
        pack_kernel,
        grid=(1,),
        in_specs=[
            pl.BlockSpec((nx, 8, nz), lambda i: (0, 0, 0)),
            pl.BlockSpec((nx, 8, nz), lambda i: (0, lines, 0)),
            pl.BlockSpec((3, nx, 8, nz), lambda i: (0, 0, 0, 0)),
            pl.BlockSpec((3, nx, 8, nz), lambda i: (0, 0, lines, 0)),
            pl.BlockSpec((4, ny, nz), lambda i: (0, 0, 0)),
            pl.BlockSpec((2, ny, nz), lambda i: (ends, 0, 0)),
            pl.BlockSpec((3, 2, ny, nz), lambda i: (0, 0, 0, 0)),
            pl.BlockSpec((3, 2, ny, nz), lambda i: (0, ends, 0, 0)),
        ],
        out_specs=[whole(side) for side in sides] + [whole(corner)] * 4,
        out_shape=[shape(*side) for side in sides] + [shape(*corner)] * 4,
        compiler_params=params(),
    )(density, density, cotangent, cotangent, density, density, cotangent, cotangent)
    steps = ((1, 0), (-1, 0), (0, 1), (0, -1), (1, 1), (1, -1), (-1, 1), (-1, -1))
    halo = [neighbours(value, *step) for value, step in zip(sent, steps)]

    pick = jnp.arange(16)[:, None, None] == jnp.arange(16).reshape(1, 2, 8)
    w_in = w_inner.T[:, None, None, :, None] * pick[None, :, :, None, :].astype(BF16)
    w_in = w_in.reshape(count * 16, 2 * hidden * 8)
    w_out = jnp.repeat(w_outer.astype(F32), 8, axis=1)

    extended = (nx + 1, ny + 8, nz)
    around = (ny + 16, nz)
    s, q, sums = pl.pallas_call(
        moments_kernel,
        out_shape=[shape(*extended), shape(*extended), shape(devices, 128)],
        scratch_shapes=[pltpu.VMEM((nx + 5,) + around, F32)]
        + [pltpu.VMEM((nx + 4,) + around, F32)] * 4
        + [pltpu.VMEM(around, F32), pltpu.VMEM((4, 8, nz), F32)],
        compiler_params=params(),
    )(density, cotangent, *halo)
    sums = collect(sums)

    half = hidden * 8
    long = ny // 8 * nz
    grad, grads = pl.pallas_call(
        closure_kernel,
        grid=(nx,),
        in_specs=[
            whole((devices, 128)), planes, whole(extended), whole(extended),
            pl.BlockSpec((count, 1, ny, nz), lambda i: (0, i, 0, 0)), whole(w_in.shape), whole(w_out.shape),
        ],
        out_specs=[planes, whole((devices, 8, 128))],
        out_shape=[shape(3, nx, ny, nz), shape(devices, 8, 128)],
        scratch_shapes=[
            pltpu.VMEM((2, 8, nz), F32),
            pltpu.VMEM((3, ny, nz), F32),
            pltpu.VMEM((long, half), BF16),
            pltpu.VMEM((long, half), BF16),
            pltpu.VMEM((32, long), BF16),
            pltpu.VMEM((24 * count, long), BF16),
            pltpu.VMEM((32, half), F32),
            pltpu.VMEM((24 * count, half), F32),
        ],
        compiler_params=params(),
    )(sums, cotangent, s, q, features, w_in, w_out)
    grads = jnp.sum(collect(grads), 0) / cells
    return grad, grads[:, :hidden].T, grads[:3, hidden:]


def solution(mesh):
    in_specs = (P("gx", "gy", None), P(None, "gx", "gy", None), P(None, "gx", "gy", None), P(), P())
    out_specs = (P(None, "gx", "gy", None), P(), P())
    return jax.shard_map(body, mesh=mesh, in_specs=in_specs, out_specs=out_specs, check_vma=False)
```

```python
import jax
import jax.numpy as jnp
from jax import lax
from jax.experimental import pallas as pl
from jax.experimental.pallas import tpu as pltpu
from jax.sharding import PartitionSpec as P

F32 = jnp.float32
BF16 = jnp.bfloat16
FIRST = (((0,), (0,)), ((), ()))
VMEM = 56 * 2**20


def collect(copies):
    return lax.all_to_all(copies, ("gx", "gy"), 0, 0)


def neighbours(value, by_x, by_y):
    nx, ny = lax.axis_size("gx"), lax.axis_size("gy")
    pairs = [
        (i * ny + j, (i + by_x) * ny + j + by_y)
        for i in range(nx)
        for j in range(ny)
        if 0 <= i + by_x < nx and 0 <= j + by_y < ny
    ]
    return lax.ppermute(value, ("gx", "gy"), pairs)


def next_lane(plane):
    size = plane.shape[1]
    at = lax.broadcasted_iota(jnp.int32, plane.shape, 1)
    return jnp.where(at == size - 1, 0.0, pltpu.roll(plane, size - 1, 1))


def prior_lane(plane):
    at = lax.broadcasted_iota(jnp.int32, plane.shape, 1)
    return jnp.where(at == 0, 0.0, pltpu.roll(plane, 1, 1))


def next_row(plane):
    return pltpu.roll(plane, plane.shape[0] - 1, 0)


def prior_row(plane):
    return pltpu.roll(plane, 1, 0)


def fold(plane):
    return jnp.sum(plane.reshape(-1, 8, plane.shape[1]), 0)


LOWER_Y = ((0, 2), (1, 1), (2, 2), (3, 1))
UPPER_Y = ((0, 3), (1, 2), (2, 2), (3, 2))


def starts(plan):
    places, at = [], 0
    for _, width in plan:
        places.append(at)
        at += width
    return places, at


def pack_kernel(d_first, d_last, c_first, c_last, up, down):
    planes = d_first.shape[0]

    def line(field, x, y):
        if field == 0:
            block = d_first if y >= 0 else d_last
            return block[x, y % 8 : y % 8 + 1, :]
        block = c_first if y >= 0 else c_last
        return block[field - 1, x, y % 8 : y % 8 + 1, :]

    for plan, to, low in ((LOWER_Y, up, False), (UPPER_Y, down, True)):
        at = 0
        for field, width in plan:
            for y in range(width):
                for x in range(planes):
                    to[at : at + 1, :] = line(field, x, y if low else y - width)
                    at += 1


def sides(below_y, above_y, planes, field, x):
    low, high, width = LOWER_Y[field][1], UPPER_Y[field][1], below_y.shape[1]
    low_at, high_at = starts(LOWER_Y)[0][field], starts(UPPER_Y)[0][field]
    below = [below_y[pl.ds((low_at + k) * planes + x, 1), :] for k in range(low)]
    above = [above_y[pl.ds((high_at + k) * planes + x, 1), :] for k in range(high)]
    below = jnp.concatenate([jnp.zeros((8 - low, width), F32)] + below, 0)
    return below, jnp.concatenate(above + [jnp.zeros((8 - high, width), F32)], 0)


def weight(value, after):
    return jnp.where(value > 0, 2.0 / (value + after), 0.0)


def across(here, beta_y, beta_z, cot_y, cot_z):
    flux_y, flux_z = beta_y * cot_y, beta_z * cot_z
    return prior_row(flux_y) - flux_y + (prior_lane(flux_z) - flux_z)


def edge_kernel(d_low, d_high, c_low, c_high, below_y, above_y, up, down):
    planes = below_y.shape[0] // starts(LOWER_Y)[1]

    def plane(field, x):
        low, high = sides(below_y, above_y, planes, field, x)
        d, c, at = (d_low, c_low, x) if x < 4 else (d_high, c_high, x - planes + 2)
        return jnp.concatenate([low, d[at] if field == 0 else c[field - 1, at], high], 0)

    def part(x):
        here = plane(0, x)
        return across(here, weight(here, next_row(here)), weight(here, next_lane(here)), plane(2, x), plane(3, x))

    last = planes - 1
    here, before = plane(0, last), plane(0, last - 1)
    up[0] = here
    up[1] = plane(1, last)
    up[2] = jnp.where(here > 0, weight(before, here) * plane(1, last - 1) + part(last), 0.0)
    here, after = plane(0, 0), plane(0, 1)
    down[0] = here
    down[1] = after
    flux = weight(here, after) * plane(1, 0)
    down[2] = jnp.where(here > 0, part(0) - flux, 0.0)
    down[3] = jnp.where(after > 0, flux - weight(after, plane(0, 2)) * plane(1, 1) + part(1), 0.0)


def moments_kernel(
    dens_far, cot_far, below_x, above_x, below_y, above_y,
    s_out, q_out, sums, dens, cot, d_all, b_x, b_y, b_z, s_all, before, acc, sems,
):
    planes, rows, width = dens.shape
    own = slice(8, rows + 8)
    part = planes // 4
    copies = [pltpu.make_async_copy(dens_far, dens, sems.at[4])]
    for k in range(4):
        span = pl.ds(k * part, part)
        copies.append(pltpu.make_async_copy(cot_far.at[:, span], cot.at[:, span], sems.at[k]))
    for copy in copies:
        copy.start()

    def fill(x, carry):
        low, high = sides(below_y, above_y, planes, 0, x)
        d_all[x + 1, 0:8, :] = low
        d_all[x + 1, own, :] = dens[x]
        d_all[x + 1, rows + 8 : rows + 16, :] = high
        return carry

    d_all[0] = below_x[0]
    d_all[planes + 1] = above_x[0]
    d_all[planes + 2] = above_x[1]
    copies[0].wait()
    lax.fori_loop(0, planes, fill, 0)

    def weights(x):
        at = x + 1
        here = d_all[at]
        b_x[at] = weight(here, d_all[at + 1])
        b_y[at] = weight(here, next_row(here))
        b_z[at] = weight(here, next_lane(here))

    def field(index, x):
        low, high = sides(below_y, above_y, planes, index, x)
        return jnp.concatenate([low, cot[index - 1, x], high], 0)

    def source(x, carry):
        at = x + 1
        here = d_all[at]
        weights(x)
        flux = b_x[at] * field(1, x)
        out = before[...] - flux + across(here, b_y[at], b_z[at], field(2, x), field(3, x))
        before[...] = flux
        s_all[at] = jnp.where(here > 0, out, 0.0)
        return carry

    b_x[0] = weight(d_all[0], d_all[1])
    flux = b_x[0] * below_x[1]
    before[...] = flux
    s_all[0] = below_x[2] - flux
    for k in range(4):
        copies[1 + k].wait()
        lax.fori_loop(k * part, (k + 1) * part, source, 0)
    s_all[planes + 1] = jnp.where(d_all[planes + 1] > 0, above_x[2] + before[...], 0.0)
    s_all[planes + 2] = above_x[3]
    weights(planes)

    def image(x):
        at = x + 1
        here = s_all[at]
        flux = b_x[at] * (s_all[at + 1] - here)
        out = before[...] - flux
        before[...] = flux
        flux = b_y[at] * (next_row(here) - here)
        out = out + (prior_row(flux) - flux)
        flux = b_z[at] * (next_lane(here) - here)
        out = out + (prior_lane(flux) - flux)
        out = jnp.where(d_all[at] > 0, out, 0.0)
        s_out[x] = here[8:]
        q_out[x] = out[8:]
        return here, out

    def squares(x, out):
        at = x + 1
        jump = (next_row(out) - out)[own]
        jump_z = next_lane(out[own]) - out[own]
        acc[3] += fold(b_y[at, own, :] * jump * jump + b_z[at, own, :] * jump_z * jump_z)

    def jumps(x, out):
        jump = out[own] - q_out[x - 1, 0:rows, :]
        acc[3] += fold(b_x[x, own, :] * jump * jump)

    def products(here, out):
        here, out = here[own], out[own]
        acc[0] += fold(here * here)
        acc[1] += fold(here * out)
        acc[2] += fold(out * out)

    before[...] = b_x[0] * (s_all[1] - s_all[0])
    acc[...] = jnp.zeros_like(acc)
    here, out = image(0)
    products(here, out)
    squares(0, out)

    def own_image(x, carry):
        here, out = image(x)
        products(here, out)
        squares(x, out)
        jumps(x, out)
        return carry

    lax.fori_loop(1, planes, own_image, 0)
    here, out = image(planes)
    jumps(planes, out)
    at = lax.broadcasted_iota(jnp.int32, (1, 128), 1)
    row = jnp.zeros((1, 128), F32)
    for k in range(4):
        value = jnp.sum(jnp.sum(acc[k], 0, keepdims=True), 1, keepdims=True)
        row = row + jnp.where(at == k, value, 0.0)
    sums[...] = jnp.broadcast_to(row, sums.shape)


def closure_kernel(
    sums, cot, s, q, feats, w_in, w_out,
    grad, grads, scale, velocity, hid, slope, vel, prod, acc_o, acc_t,
):
    step, planes = pl.program_id(0), s.shape[0] - 1
    rows, width = cot.shape[2], s.shape[2]
    count = feats.shape[0]

    @pl.when(step == 0)
    def _():
        all_sums = jnp.sum(sums[...], 0, keepdims=True)
        at_lane = lax.broadcasted_iota(jnp.int32, (1, 128), 1)
        m0, m1, m2, m3 = (
            jnp.sum(jnp.where(at_lane == k, all_sums, 0.0), 1, keepdims=True) for k in range(4)
        )
        alpha0 = m0 / m1
        rr1 = alpha0 * alpha0 * m2 - m0
        beta = rr1 / m0
        more = 1.0 + beta
        alpha1 = rr1 / (more * more * m1 - 2.0 * more * alpha0 * m2 + alpha0 * alpha0 * m3)
        scale[0] = jnp.broadcast_to(alpha0 + alpha1 * more, scale.shape[1:])
        scale[1] = jnp.broadcast_to(-alpha1 * alpha0, scale.shape[1:])
        acc_o[...] = jnp.zeros_like(acc_o)
        acc_t[...] = jnp.zeros_like(acc_t)

    on_s, on_q = scale[0][:1], scale[1][:1]
    last = step == planes - 1
    wide = on_s * s[step] + on_q * q[step]
    here = wide[:rows]
    beyond = on_s * s[step + 1, :rows, :] + on_q * q[step + 1, :rows, :]
    for a, after in enumerate((beyond, next_row(wide)[:rows], next_lane(here))):
        value = cot[a, 0] - (after - here)
        grad[a, 0] = value
        velocity[a] = value.astype(BF16).astype(F32)

    half = w_in.shape[1] // 2
    blocks, wide_tile = rows // 16, 256

    def place(block, tile):
        part, column = divmod(tile * wide_tile, half)
        cells = (block * 2 + part) * width
        return slice(cells, cells + width), slice(column, column + wide_tile)

    def first_layer(block, tile):
        inner = feats[:, 0, block * 16 : block * 16 + 16, :].reshape(count * 16, width)
        weights = w_in[:, tile * wide_tile : (tile + 1) * wide_tile]
        pre = lax.dot_general(inner, weights, FIRST, preferred_element_type=F32)
        hidden = jnp.tanh(pre)
        to = place(block, tile)
        hid[to] = hidden.astype(BF16)
        slope[to] = (1.0 - hidden * hidden).astype(BF16)

    def outer(block, tile):
        cells, columns = place(block, tile)
        acc_o[:, columns] += jnp.dot(vel[:, cells], hid[cells, columns], preferred_element_type=F32)

    for block in range(blocks):
        at = slice(block * 16, block * 16 + 16)
        broad = [feats[c, 0, at, :].astype(F32) for c in range(count)]
        for part in range(2):
            to = slice((block * 2 + part) * width, (block * 2 + part + 1) * width)
            low = block * 16 + part * 8
            vs = [velocity[a, low : low + 8, :] for a in range(3)]
            vel[:, to] = jnp.concatenate(vs + [jnp.zeros_like(vs[0])], 0).astype(BF16)
            fs = [f[part * 8 : part * 8 + 8] for f in broad]
            prod[:, to] = jnp.concatenate([v * f for v in vs for f in fs], 0).astype(BF16)
    tiles = w_in.shape[1] // wide_tile
    late = 2
    for block in range(blocks + late):
        for tile in range(tiles):
            if block < blocks:
                first_layer(block, tile)
            if block >= late:
                outer(block - late, tile)
    acc_t[...] += jnp.dot(prod[...], slope[...], preferred_element_type=F32)

    @pl.when(last)
    def _():
        def own(value):
            at_row = lax.broadcasted_iota(jnp.int32, value.shape, 0) % 8
            at_col = lax.broadcasted_iota(jnp.int32, value.shape, 1) % 8
            kept = jnp.where(at_row == at_col, value, 0.0)
            return jnp.sum(kept.reshape(-1, 8, value.shape[1]), 1)

        outermost = own(acc_o[...])
        terms = own(acc_t[...])
        inner = sum(
            w_out[a : a + 1] * terms[a * count : (a + 1) * count] for a in range(3)
        )
        both = jnp.concatenate([inner, outermost[:3], jnp.zeros((5, half), F32)], 0)
        hidden_at = lax.broadcasted_iota(jnp.int32, (half, 64), 0) // 8
        column = lax.broadcasted_iota(jnp.int32, (half, 64), 1)
        pick = (hidden_at == column).astype(F32)
        sums16 = jnp.dot(both, pick, precision=lax.Precision.HIGHEST, preferred_element_type=F32)
        value = jnp.concatenate([sums16[:8], sums16[8:]], 1)
        grads[...] = jnp.broadcast_to(value[None], grads.shape)


def whole(shape):
    return pl.BlockSpec(shape, lambda i: (0,) * len(shape))


def shape(*dims):
    return jax.ShapeDtypeStruct(dims, F32)


def params():
    return pltpu.CompilerParams(vmem_limit_bytes=VMEM)


def body(density, cotangent, features, w_inner, w_outer):
    nx, ny, nz = density.shape
    count, hidden = features.shape[0], w_inner.shape[0]
    devices = lax.axis_size("gx") * lax.axis_size("gy")
    cells = float(density.size * devices)
    planes = pl.BlockSpec((3, 1, ny, nz), lambda i: (0, i, 0, 0))
    lines, ends = ny // 8 - 1, nx // 2 - 1
    around = (ny + 16, nz)
    to_up, to_down = pl.pallas_call(
        pack_kernel,
        grid=(1,),
        in_specs=[
            pl.BlockSpec((nx, 8, nz), lambda i: (0, 0, 0)),
            pl.BlockSpec((nx, 8, nz), lambda i: (0, lines, 0)),
            pl.BlockSpec((3, nx, 8, nz), lambda i: (0, 0, 0, 0)),
            pl.BlockSpec((3, nx, 8, nz), lambda i: (0, 0, lines, 0)),
        ],
        out_specs=[whole((starts(plan)[1] * nx, nz)) for plan in (LOWER_Y, UPPER_Y)],
        out_shape=[shape(starts(plan)[1] * nx, nz) for plan in (LOWER_Y, UPPER_Y)],
        compiler_params=params(),
    )(density, density, cotangent, cotangent)
    below_y, above_y = neighbours(to_up, 0, 1), neighbours(to_down, 0, -1)
    to_up, to_down = pl.pallas_call(
        edge_kernel,
        grid=(1,),
        in_specs=[
            pl.BlockSpec((4, ny, nz), lambda i: (0, 0, 0)),
            pl.BlockSpec((2, ny, nz), lambda i: (ends, 0, 0)),
            pl.BlockSpec((3, 2, ny, nz), lambda i: (0, 0, 0, 0)),
            pl.BlockSpec((3, 2, ny, nz), lambda i: (0, ends, 0, 0)),
            whole(below_y.shape),
            whole(above_y.shape),
        ],
        out_specs=[whole((3,) + around), whole((4,) + around)],
        out_shape=[shape(3, *around), shape(4, *around)],
        compiler_params=params(),
    )(density, density, cotangent, cotangent, below_y, above_y)
    halo = [neighbours(to_up, 1, 0), neighbours(to_down, -1, 0), below_y, above_y]

    pick = jnp.arange(16)[:, None, None] == jnp.arange(16).reshape(1, 2, 8)
    w_in = w_inner.T[:, None, None, :, None] * pick[None, :, :, None, :].astype(BF16)
    w_in = w_in.reshape(count * 16, 2 * hidden * 8)
    w_out = jnp.repeat(w_outer.astype(F32), 8, axis=1)

    extended = (nx + 1, ny + 8, nz)
    anywhere = pl.BlockSpec(memory_space=pl.ANY)
    near = pl.BlockSpec(memory_space=pltpu.VMEM)
    s, q, sums = pl.pallas_call(
        moments_kernel,
        in_specs=[anywhere] * 2 + [near] * 4,
        out_shape=[shape(*extended), shape(*extended), shape(devices, 128)],
        scratch_shapes=[pltpu.VMEM((nx, ny, nz), F32), pltpu.VMEM((3, nx, ny, nz), F32)]
        + [pltpu.VMEM((nx + 3,) + around, F32)]
        + [pltpu.VMEM((nx + 2,) + around, F32)] * 3
        + [pltpu.VMEM((nx + 3,) + around, F32)]
        + [pltpu.VMEM(around, F32), pltpu.VMEM((4, 8, nz), F32), pltpu.SemaphoreType.DMA((5,))],
        compiler_params=params(),
    )(density, cotangent, *halo)
    sums = collect(sums)

    half = hidden * 8
    long = ny // 8 * nz
    grad, grads = pl.pallas_call(
        closure_kernel,
        grid=(nx,),
        in_specs=[
            whole((devices, 128)), planes, whole(extended), whole(extended),
            pl.BlockSpec((count, 1, ny, nz), lambda i: (0, i, 0, 0)), whole(w_in.shape), whole(w_out.shape),
        ],
        out_specs=[planes, whole((devices, 8, 128))],
        out_shape=[shape(3, nx, ny, nz), shape(devices, 8, 128)],
        scratch_shapes=[
            pltpu.VMEM((2, 8, nz), F32),
            pltpu.VMEM((3, ny, nz), F32),
            pltpu.VMEM((long, half), BF16),
            pltpu.VMEM((long, half), BF16),
            pltpu.VMEM((32, long), BF16),
            pltpu.VMEM((24 * count, long), BF16),
            pltpu.VMEM((32, half), F32),
            pltpu.VMEM((24 * count, half), F32),
        ],
        compiler_params=params(),
    )(sums, cotangent, s, q, features, w_in, w_out)
    grads = jnp.sum(collect(grads), 0) / cells
    return grad, grads[:, :hidden].T, grads[:3, hidden:]


def solution(mesh):
    in_specs = (P("gx", "gy", None), P(None, "gx", "gy", None), P(None, "gx", "gy", None), P(), P())
    out_specs = (P(None, "gx", "gy", None), P(), P())
    return jax.shard_map(body, mesh=mesh, in_specs=in_specs, out_specs=out_specs, check_vma=False)
```

```python
import jax
import jax.numpy as jnp
from jax import lax
from jax.experimental import pallas as pl
from jax.experimental.pallas import tpu as pltpu
from jax.sharding import PartitionSpec as P

F32 = jnp.float32
BF16 = jnp.bfloat16
FIRST = (((0,), (0,)), ((), ()))
LAST = (((1,), (1,)), ((), ()))


def collect(copies):
    return lax.all_to_all(copies, ("gx", "gy"), 0, 0)


def neighbours(value, by_x, by_y):
    nx, ny = lax.axis_size("gx"), lax.axis_size("gy")
    pairs = [
        (i * ny + j, (i + by_x) * ny + j + by_y)
        for i in range(nx)
        for j in range(ny)
        if 0 <= i + by_x < nx and 0 <= j + by_y < ny
    ]
    return lax.ppermute(value, ("gx", "gy"), pairs)


def next_lane(plane):
    size = plane.shape[1]
    at = lax.broadcasted_iota(jnp.int32, plane.shape, 1)
    return jnp.where(at == size - 1, 0.0, pltpu.roll(plane, size - 1, 1))


def prior_lane(plane):
    at = lax.broadcasted_iota(jnp.int32, plane.shape, 1)
    return jnp.where(at == 0, 0.0, pltpu.roll(plane, 1, 1))


def next_row(plane):
    return pltpu.roll(plane, plane.shape[0] - 1, 0)


def prior_row(plane):
    return pltpu.roll(plane, 1, 0)


def fold(plane):
    return jnp.sum(plane.reshape(-1, 8, plane.shape[1]), 0)


LOWER_Y = ((0, 2), (1, 1), (2, 2), (3, 1))
UPPER_Y = ((0, 3), (1, 2), (2, 2), (3, 2))


def starts(plan):
    places, at = [], 0
    for _, width in plan:
        places.append(at)
        at += width
    return places, at


def pack_kernel(d_first, d_last, c_first, c_last, up, down):
    planes = d_first.shape[0]

    def line(field, x, y):
        if field == 0:
            block = d_first if y >= 0 else d_last
            return block[x, y % 8 : y % 8 + 1, :]
        block = c_first if y >= 0 else c_last
        return block[field - 1, x, y % 8 : y % 8 + 1, :]

    for plan, to, low in ((LOWER_Y, up, False), (UPPER_Y, down, True)):
        at = 0
        for field, width in plan:
            for y in range(width):
                for x in range(planes):
                    to[at : at + 1, :] = line(field, x, y if low else y - width)
                    at += 1


def sides(below_y, above_y, planes, field, x):
    low, high, width = LOWER_Y[field][1], UPPER_Y[field][1], below_y.shape[1]
    low_at, high_at = starts(LOWER_Y)[0][field], starts(UPPER_Y)[0][field]
    below = [below_y[pl.ds((low_at + k) * planes + x, 1), :] for k in range(low)]
    above = [above_y[pl.ds((high_at + k) * planes + x, 1), :] for k in range(high)]
    below = jnp.concatenate([jnp.zeros((8 - low, width), F32)] + below, 0)
    return below, jnp.concatenate(above + [jnp.zeros((8 - high, width), F32)], 0)


def weight(value, after):
    return jnp.where(value > 0, 2.0 / (value + after), 0.0)


def across(here, beta_y, beta_z, cot_y, cot_z):
    flux_y, flux_z = beta_y * cot_y, beta_z * cot_z
    return prior_row(flux_y) - flux_y + (prior_lane(flux_z) - flux_z)


def edge_kernel(d_low, d_high, c_low, c_high, below_y, above_y, up, down):
    planes = below_y.shape[0] // starts(LOWER_Y)[1]

    def plane(field, x):
        low, high = sides(below_y, above_y, planes, field, x)
        d, c, at = (d_low, c_low, x) if x < 4 else (d_high, c_high, x - planes + 2)
        return jnp.concatenate([low, d[at] if field == 0 else c[field - 1, at], high], 0)

    def part(x):
        here = plane(0, x)
        return across(here, weight(here, next_row(here)), weight(here, next_lane(here)), plane(2, x), plane(3, x))

    last = planes - 1
    here, before = plane(0, last), plane(0, last - 1)
    up[0] = here
    up[1] = plane(1, last)
    up[2] = jnp.where(here > 0, weight(before, here) * plane(1, last - 1) + part(last), 0.0)
    here, after = plane(0, 0), plane(0, 1)
    down[0] = here
    down[1] = after
    flux = weight(here, after) * plane(1, 0)
    down[2] = jnp.where(here > 0, part(0) - flux, 0.0)
    down[3] = jnp.where(after > 0, flux - weight(after, plane(0, 2)) * plane(1, 1) + part(1), 0.0)


def source_kernel(
    dens_far, cot_far, below_y, above_y, s_part, b_x, b_y, b_z, dens, cot, d_all, before, sems
):
    planes, rows, width = dens.shape
    part = planes // 4
    copies = [pltpu.make_async_copy(dens_far, dens, sems.at[4])]
    for k in range(4):
        span = pl.ds(k * part, part)
        copies.append(pltpu.make_async_copy(cot_far.at[:, span], cot.at[:, span], sems.at[k]))
    for copy in copies:
        copy.start()

    def fill(x, carry):
        low, high = sides(below_y, above_y, planes, 0, x)
        d_all[x, 0:8, :] = low
        d_all[x, 8 : rows + 8, :] = dens[x]
        d_all[x, rows + 8 : rows + 16, :] = high
        return carry

    def field(index, x):
        low, high = sides(below_y, above_y, planes, index, x)
        return jnp.concatenate([low, cot[index - 1, x], high], 0)

    def rest(x, here):
        b_y[x] = weight(here, next_row(here))
        b_z[x] = weight(here, next_lane(here))
        return across(here, b_y[x], b_z[x], field(2, x), field(3, x))

    def source(x, carry):
        here = d_all[x]
        b_x[x] = weight(here, d_all[x + 1])
        flux = b_x[x] * field(1, x)
        out = before[...] - flux + rest(x, here)
        before[...] = flux
        s_part[x] = jnp.where(here > 0, out, 0.0)
        return carry

    copies[0].wait()
    lax.fori_loop(0, planes, fill, 0)
    before[...] = jnp.zeros_like(before)
    for k in range(4):
        copies[1 + k].wait()
        lax.fori_loop(k * part, min((k + 1) * part, planes - 1), source, 0)
    here = d_all[planes - 1]
    b_x[planes - 1] = jnp.zeros_like(here)
    s_part[planes - 1] = jnp.where(here > 0, before[...] + rest(planes - 1, here), 0.0)


def moments_kernel(
    below_x, above_x, own_up, own_down, s_part, b_x, b_y, b_z,
    s_far, q_far, sums, s_out, q_out, first, final, b_final, before, acc, sems,
):
    planes, width = s_part.shape[0], s_part.shape[2]
    rows = s_part.shape[1] - 16
    own = slice(8, rows + 8)
    last = planes - 1
    beta = weight(below_x[0], own_down[0])
    flux = beta * below_x[1]
    first[...] = s_part[0] + flux
    before[...] = beta * (first[...] - (below_x[2] - flux))
    b_final[...] = weight(own_up[0], above_x[0])
    flux = b_final[...] * own_up[1]
    final[...] = s_part[last] - flux
    s_after = jnp.where(above_x[0] > 0, above_x[2] + flux, 0.0)

    def leaving(x):
        return (
            pltpu.make_async_copy(s_out.at[x], s_far.at[x], sems.at[0, x]),
            pltpu.make_async_copy(q_out.at[x], q_far.at[x], sems.at[1, x]),
        )

    def image(x, here, after, beta_x, beta_y, beta_z):
        flux = beta_x * (after - here)
        out = before[...] - flux
        before[...] = flux
        flux = beta_y * (next_row(here) - here)
        out = out + (prior_row(flux) - flux)
        flux = beta_z * (next_lane(here) - here)
        out = out + (prior_lane(flux) - flux)
        out = jnp.where(beta_y > 0, out, 0.0)
        s_out[x] = here[8:]
        q_out[x] = out[8:]
        for copy in leaving(x):
            copy.start()
        return here, out

    def jumps(x, out, beta_x):
        jump = out[own] - q_out[x - 1, 0:rows, :]
        acc[3] += fold(beta_x * jump * jump)

    def products(x, here, out):
        jump = (next_row(out) - out)[own]
        here, out = here[own], out[own]
        jump_z = next_lane(out) - out
        acc[3] += fold(b_y[x, own, :] * jump * jump + b_z[x, own, :] * jump_z * jump_z)
        acc[0] += fold(here * here)
        acc[1] += fold(here * out)
        acc[2] += fold(out * out)

    acc[...] = jnp.zeros_like(acc)
    products(0, *image(0, first[...], s_part[1], b_x[0], b_y[0], b_z[0]))

    def inside(x, carry):
        here, out = image(x, s_part[x], s_part[x + 1], b_x[x], b_y[x], b_z[x])
        products(x, here, out)
        jumps(x, out, b_x[x - 1, own, :])
        return carry

    lax.fori_loop(1, last - 1, inside, 0)
    here, out = image(last - 1, s_part[last - 1], final[...], b_x[last - 1], b_y[last - 1], b_z[last - 1])
    products(last - 1, here, out)
    jumps(last - 1, out, b_x[last - 2, own, :])
    here, out = image(last, final[...], s_after, b_final[...], b_y[last], b_z[last])
    products(last, here, out)
    jumps(last, out, b_x[last - 1, own, :])
    after = above_x[0]
    betas = weight(after, above_x[1]), weight(after, next_row(after)), weight(after, next_lane(after))
    here, out = image(planes, s_after, above_x[3], *betas)
    jumps(planes, out, b_final[own, :])
    at = lax.broadcasted_iota(jnp.int32, (1, 128), 1)
    row = jnp.zeros((1, 128), F32)
    for k in range(4):
        value = jnp.sum(jnp.sum(acc[k], 0, keepdims=True), 1, keepdims=True)
        row = row + jnp.where(at == k, value, 0.0)
    sums[...] = jnp.broadcast_to(row, sums.shape)
    for x in range(planes + 1):
        for copy in leaving(x):
            copy.wait()


def spreading(columns):
    at_column = lax.broadcasted_iota(jnp.int32, (64, columns), 1)
    return (at_column // 8 % 64 == lax.broadcasted_iota(jnp.int32, (64, columns), 0)).astype(F32)


def closure_kernel(
    sums, cot, s, q, s_next, q_next, feats, w_inner, w_outer,
    grad, grads, w_in, scale, velocity, hid, slope, vel, prod, acc_o, acc_t,
):
    step, planes = pl.program_id(0), cot.shape[1]
    rows, width = cot.shape[2], cot.shape[3]
    count = feats.shape[0]

    @pl.when(step == 0)
    def _():
        all_sums = jnp.sum(sums[...], 0, keepdims=True)
        at_lane = lax.broadcasted_iota(jnp.int32, (1, 128), 1)
        m0, m1, m2, m3 = (
            jnp.sum(jnp.where(at_lane == k, all_sums, 0.0), 1, keepdims=True) for k in range(4)
        )
        alpha0 = m0 / m1
        rr1 = alpha0 * alpha0 * m2 - m0
        beta = rr1 / m0
        more = 1.0 + beta
        alpha1 = rr1 / (more * more * m1 - 2.0 * more * alpha0 * m2 + alpha0 * alpha0 * m3)
        scale[0] = jnp.broadcast_to(alpha0 + alpha1 * more, scale.shape[1:])
        scale[1] = jnp.broadcast_to(-alpha1 * alpha0, scale.shape[1:])
        acc_o[...] = jnp.zeros_like(acc_o)
        acc_t[...] = jnp.zeros_like(acc_t)
        at_row, at_column = (lax.broadcasted_iota(jnp.int32, w_in.shape, k) for k in range(2))
        pick = lax.broadcasted_iota(jnp.int32, (w_in.shape[0], count), 0) // 16
        pick = (pick == lax.broadcasted_iota(jnp.int32, pick.shape, 1)).astype(BF16)
        tall = lax.dot_general(pick, w_inner[...], LAST, preferred_element_type=F32).astype(BF16)
        spread = jnp.dot(tall, spreading(w_in.shape[1]).astype(BF16), preferred_element_type=F32)
        same = at_row % 16 == at_column // (w_in.shape[1] // 2) * 8 + at_column % 8
        w_in[...] = jnp.where(same, spread, 0.0).astype(BF16)

    on_s, on_q = scale[0][:1], scale[1][:1]
    last = step == pl.num_programs(0) - 1
    beyond = on_s * s[0] + on_q * q[0]
    for x in range(planes):
        wide = beyond
        if x + 1 < planes:
            beyond = on_s * s[x + 1] + on_q * q[x + 1]
        else:
            beyond = on_s * s_next[0] + on_q * q_next[0]
        here = wide[:rows]
        for a, after in enumerate((beyond[:rows], next_row(wide)[:rows], next_lane(here))):
            value = cot[a, x] - (after - here)
            grad[a, x] = value
            velocity[a, x] = value.astype(BF16).astype(F32)

    half = w_in.shape[1] // 2
    per_plane, wide_tile = rows // 16, 256
    blocks = planes * per_plane

    def place_of(block):
        x, at = divmod(block, per_plane)
        return x, slice(at * 16, at * 16 + 16)

    def place(block, tile):
        part, column = divmod(tile * wide_tile, half)
        cells = (block * 2 + part) * width
        return slice(cells, cells + width), slice(column, column + wide_tile)

    def first_layer(block, tile):
        x, at = place_of(block)
        inner = feats[:, x, at, :].reshape(count * 16, width)
        weights = w_in[:, tile * wide_tile : (tile + 1) * wide_tile]
        pre = lax.dot_general(inner, weights, FIRST, preferred_element_type=F32)
        hidden = jnp.tanh(pre)
        to = place(block, tile)
        hid[to] = hidden.astype(BF16)
        slope[to] = (1.0 - hidden * hidden).astype(BF16)

    def outer(block, tile):
        cells, columns = place(block, tile)
        acc_o[:, columns] += jnp.dot(vel[:, cells], hid[cells, columns], preferred_element_type=F32)

    for block in range(blocks):
        x, at = place_of(block)
        broad = [feats[c, x, at, :].astype(F32) for c in range(count)]
        for part in range(2):
            to = slice((block * 2 + part) * width, (block * 2 + part + 1) * width)
            low = at.start + part * 8
            vs = [velocity[a, x, low : low + 8, :] for a in range(3)]
            vel[:, to] = jnp.concatenate(vs + [jnp.zeros_like(vs[0])], 0).astype(BF16)
            fs = [f[part * 8 : part * 8 + 8] for f in broad]
            prod[:, to] = jnp.concatenate([v * f for v in vs for f in fs], 0).astype(BF16)
    tiles = w_in.shape[1] // wide_tile
    late = 2
    for block in range(blocks + late):
        for tile in range(tiles):
            if block < blocks:
                first_layer(block, tile)
            if block >= late:
                outer(block - late, tile)
    acc_t[...] += jnp.dot(prod[...], slope[...], preferred_element_type=F32)

    @pl.when(last)
    def _():
        def own(value):
            at_row = lax.broadcasted_iota(jnp.int32, value.shape, 0) % 8
            at_col = lax.broadcasted_iota(jnp.int32, value.shape, 1) % 8
            kept = jnp.where(at_row == at_col, value, 0.0)
            return jnp.sum(kept.reshape(-1, 8, value.shape[1]), 1)

        outermost = own(acc_o[...])
        terms = own(acc_t[...])
        w_out = jnp.dot(w_outer[...], spreading(half).astype(BF16), preferred_element_type=F32)
        inner = sum(
            w_out[a : a + 1] * terms[a * count : (a + 1) * count] for a in range(3)
        )
        both = jnp.concatenate([inner, outermost[:3], jnp.zeros((5, half), F32)], 0)
        hidden_at = lax.broadcasted_iota(jnp.int32, (half, 64), 0) // 8
        column = lax.broadcasted_iota(jnp.int32, (half, 64), 1)
        pick = (hidden_at == column).astype(F32)
        sums16 = jnp.dot(both, pick, precision=lax.Precision.HIGHEST, preferred_element_type=F32)
        value = [sums16[k : k + 1] for k in (0, 4, 1, 5, 2, 6, 3, 7, 8, 10, 9, 11)]
        grads[...] = jnp.broadcast_to(jnp.concatenate(value, 1)[None], grads.shape)


def whole(shape):
    return pl.BlockSpec(shape, lambda i: (0,) * len(shape))


def shape(*dims):
    return jax.ShapeDtypeStruct(dims, F32)


def held(*dims):
    return pltpu.VMEM(dims, F32)


def keep(value):
    return pltpu.with_memory_space_constraint(value, pltpu.VMEM)


def away(value):
    return pltpu.with_memory_space_constraint(value, pltpu.HBM)


def params(mebibytes=24):
    return pltpu.CompilerParams(vmem_limit_bytes=mebibytes * 2**20)


def body(density, cotangent, features, w_inner, w_outer):
    nx, ny, nz = density.shape
    count, hidden = features.shape[0], w_inner.shape[0]
    density, cotangent, features = map(away, (density, cotangent, features))
    devices = lax.axis_size("gx") * lax.axis_size("gy")
    cells = float(density.size * devices)
    lines, ends = ny // 8 - 1, nx // 2 - 1
    around = (ny + 16, nz)
    to_up, to_down = pl.pallas_call(
        pack_kernel,
        grid=(1,),
        in_specs=[
            pl.BlockSpec((nx, 8, nz), lambda i: (0, 0, 0)),
            pl.BlockSpec((nx, 8, nz), lambda i: (0, lines, 0)),
            pl.BlockSpec((3, nx, 8, nz), lambda i: (0, 0, 0, 0)),
            pl.BlockSpec((3, nx, 8, nz), lambda i: (0, 0, lines, 0)),
        ],
        out_specs=[whole((starts(plan)[1] * nx, nz)) for plan in (LOWER_Y, UPPER_Y)],
        out_shape=[shape(starts(plan)[1] * nx, nz) for plan in (LOWER_Y, UPPER_Y)],
        compiler_params=params(),
    )(density, density, cotangent, cotangent)
    below_y, above_y = neighbours(to_up, 0, 1), neighbours(to_down, 0, -1)
    to_up, to_down = pl.pallas_call(
        edge_kernel,
        grid=(1,),
        in_specs=[
            pl.BlockSpec((4, ny, nz), lambda i: (0, 0, 0)),
            pl.BlockSpec((2, ny, nz), lambda i: (ends, 0, 0)),
            pl.BlockSpec((3, 2, ny, nz), lambda i: (0, 0, 0, 0)),
            pl.BlockSpec((3, 2, ny, nz), lambda i: (0, ends, 0, 0)),
            whole(below_y.shape),
            whole(above_y.shape),
        ],
        out_specs=[whole((3,) + around), whole((4,) + around)],
        out_shape=[shape(3, *around), shape(4, *around)],
        compiler_params=params(),
    )(density, density, cotangent, cotangent, keep(below_y), keep(above_y))
    below_x, above_x = neighbours(to_up, 1, 0), neighbours(to_down, -1, 0)

    extended = (nx + 1, ny + 8, nz)
    anywhere = pl.BlockSpec(memory_space=pl.ANY)
    near = pl.BlockSpec(memory_space=pltpu.VMEM)
    whole_planes = (nx,) + around
    fields = pl.pallas_call(
        source_kernel,
        in_specs=[anywhere] * 2 + [near] * 2,
        out_shape=[held(*whole_planes)] * 4,
        scratch_shapes=[
            pltpu.VMEM((nx, ny, nz), F32),
            pltpu.VMEM((3, nx, ny, nz), F32),
            pltpu.VMEM(whole_planes, F32),
            pltpu.VMEM(around, F32),
            pltpu.SemaphoreType.DMA((5,)),
        ],
        compiler_params=params(30),
    )(density, cotangent, keep(below_y), keep(above_y))
    s, q, sums = pl.pallas_call(
        moments_kernel,
        in_specs=[near] * 8,
        out_specs=[pl.BlockSpec(memory_space=pltpu.HBM)] * 2 + [near],
        out_shape=[pltpu.HBM(extended, F32)] * 2 + [held(devices, 128)],
        scratch_shapes=[pltpu.VMEM(extended, F32)] * 2
        + [pltpu.VMEM(around, F32)] * 4
        + [pltpu.VMEM((4, 8, nz), F32), pltpu.SemaphoreType.DMA((2, nx + 1))],
        compiler_params=params(30),
    )(keep(below_x), keep(above_x), keep(to_up), keep(to_down), *fields)
    sums = collect(sums)

    half = hidden * 8
    step = 2
    long = step * ny // 8 * nz
    planes = pl.BlockSpec((3, step, ny, nz), lambda i: (0, i, 0, 0))
    here = pl.BlockSpec((step, ny + 8, nz), lambda i: (i, 0, 0))
    after = pl.BlockSpec((1, ny + 8, nz), lambda i: (step * i + step, 0, 0))
    grad, grads = pl.pallas_call(
        closure_kernel,
        grid=(nx // step,),
        in_specs=[
            whole((devices, 128)), planes, here, here, after, after,
            pl.BlockSpec((count, step, ny, nz), lambda i: (0, i, 0, 0)), whole(w_inner.shape), whole(w_outer.shape),
        ],
        out_specs=[planes, whole((devices, 1, 768))],
        out_shape=[shape(3, nx, ny, nz), shape(devices, 1, 768)],
        scratch_shapes=[
            pltpu.VMEM((count * 16, 2 * half), BF16),
            pltpu.VMEM((2, 8, nz), F32),
            pltpu.VMEM((3, step, ny, nz), F32),
            pltpu.VMEM((long, half), BF16),
            pltpu.VMEM((long, half), BF16),
            pltpu.VMEM((32, long), BF16),
            pltpu.VMEM((24 * count, long), BF16),
            pltpu.VMEM((32, half), F32),
            pltpu.VMEM((24 * count, half), F32),
        ],
        compiler_params=params(48),
    )(keep(sums), cotangent, *map(away, (s, q, s, q)), features, w_inner, w_outer)
    grads = jnp.sum(collect(grads), 0).reshape(6, 128) / cells
    low, high = grads[:, :hidden], grads[:, hidden:]
    return grad, jnp.concatenate([low[:4], high[:4]]).T, jnp.concatenate([low[4:], high[4:5]])


def solution(mesh):
    in_specs = (P("gx", "gy", None), P(None, "gx", "gy", None), P(None, "gx", "gy", None), P(), P())
    out_specs = (P(None, "gx", "gy", None), P(), P())
    return jax.shard_map(body, mesh=mesh, in_specs=in_specs, out_specs=out_specs, check_vma=False)
```

```python
import jax
import jax.numpy as jnp
from jax import lax
from jax.experimental import pallas as pl
from jax.experimental.pallas import tpu as pltpu
from jax.sharding import PartitionSpec as P

F32 = jnp.float32
BF16 = jnp.bfloat16
FIRST = (((0,), (0,)), ((), ()))
LAST = (((1,), (1,)), ((), ()))


def collect(copies):
    return lax.all_to_all(copies, ("gx", "gy"), 0, 0)


def neighbours(value, by_x, by_y):
    nx, ny = lax.axis_size("gx"), lax.axis_size("gy")
    pairs = [
        (i * ny + j, (i + by_x) * ny + j + by_y)
        for i in range(nx)
        for j in range(ny)
        if 0 <= i + by_x < nx and 0 <= j + by_y < ny
    ]
    return lax.ppermute(value, ("gx", "gy"), pairs)


def next_lane(plane):
    size = plane.shape[1]
    at = lax.broadcasted_iota(jnp.int32, plane.shape, 1)
    return jnp.where(at == size - 1, 0.0, pltpu.roll(plane, size - 1, 1))


def prior_lane(plane):
    at = lax.broadcasted_iota(jnp.int32, plane.shape, 1)
    return jnp.where(at == 0, 0.0, pltpu.roll(plane, 1, 1))


def next_row(plane):
    return pltpu.roll(plane, plane.shape[0] - 1, 0)


def prior_row(plane):
    return pltpu.roll(plane, 1, 0)


def fold(plane):
    return jnp.sum(plane.reshape(-1, 8, plane.shape[1]), 0)


LOWER_Y = ((0, 2), (1, 1), (2, 2), (3, 1))
UPPER_Y = ((0, 3), (1, 2), (2, 2), (3, 2))


def starts(plan):
    places, at = [], 0
    for _, width in plan:
        places.append(at)
        at += width
    return places, at


def pack_kernel(d_first, d_last, c_first, c_last, up, down):
    planes = d_first.shape[0]

    def line(field, x, y):
        if field == 0:
            block = d_first if y >= 0 else d_last
            return block[x, y % 8 : y % 8 + 1, :]
        block = c_first if y >= 0 else c_last
        return block[field - 1, x, y % 8 : y % 8 + 1, :]

    for plan, to, low in ((LOWER_Y, up, False), (UPPER_Y, down, True)):
        at = 0
        for field, width in plan:
            for y in range(width):
                for x in range(planes):
                    to[at : at + 1, :] = line(field, x, y if low else y - width)
                    at += 1


def sides(below_y, above_y, planes, field, x):
    low, high, width = LOWER_Y[field][1], UPPER_Y[field][1], below_y.shape[1]
    low_at, high_at = starts(LOWER_Y)[0][field], starts(UPPER_Y)[0][field]
    below = [below_y[pl.ds((low_at + k) * planes + x, 1), :] for k in range(low)]
    above = [above_y[pl.ds((high_at + k) * planes + x, 1), :] for k in range(high)]
    below = jnp.concatenate([jnp.zeros((8 - low, width), F32)] + below, 0)
    return below, jnp.concatenate(above + [jnp.zeros((8 - high, width), F32)], 0)


def weight(value, after):
    return jnp.where(value > 0, 2.0 / (value + after), 0.0)


def across(here, beta_y, beta_z, cot_y, cot_z):
    flux_y, flux_z = beta_y * cot_y, beta_z * cot_z
    return prior_row(flux_y) - flux_y + (prior_lane(flux_z) - flux_z)


def edge_kernel(dens, cot, below_y, above_y, up, down):
    planes = dens.shape[0]

    def plane(field, x):
        low, high = sides(below_y, above_y, planes, field, x)
        return jnp.concatenate([low, dens[x] if field == 0 else cot[field - 1, x], high], 0)

    def part(x):
        here = plane(0, x)
        return across(here, weight(here, next_row(here)), weight(here, next_lane(here)), plane(2, x), plane(3, x))

    last = planes - 1
    here, before = plane(0, last), plane(0, last - 1)
    up[0] = here
    up[1] = plane(1, last)
    up[2] = jnp.where(here > 0, weight(before, here) * plane(1, last - 1) + part(last), 0.0)
    here, after = plane(0, 0), plane(0, 1)
    down[0] = here
    down[1] = after
    flux = weight(here, after) * plane(1, 0)
    down[2] = jnp.where(here > 0, part(0) - flux, 0.0)
    down[3] = jnp.where(after > 0, flux - weight(after, plane(0, 2)) * plane(1, 1) + part(1), 0.0)


def source_kernel(
    dens, cot, below_y, above_y, s_part, b_x, b_y, b_z, d_all, before
):
    planes, rows, width = dens.shape

    def fill(x, carry):
        low, high = sides(below_y, above_y, planes, 0, x)
        d_all[x, 0:8, :] = low
        d_all[x, 8 : rows + 8, :] = dens[x]
        d_all[x, rows + 8 : rows + 16, :] = high
        return carry

    def field(index, x):
        low, high = sides(below_y, above_y, planes, index, x)
        return jnp.concatenate([low, cot[index - 1, x], high], 0)

    def rest(x, here):
        b_y[x] = weight(here, next_row(here))
        b_z[x] = weight(here, next_lane(here))
        return across(here, b_y[x], b_z[x], field(2, x), field(3, x))

    def source(x, carry):
        here = d_all[x]
        b_x[x] = weight(here, d_all[x + 1])
        flux = b_x[x] * field(1, x)
        out = before[...] - flux + rest(x, here)
        before[...] = flux
        s_part[x] = jnp.where(here > 0, out, 0.0)
        return carry

    lax.fori_loop(0, planes, fill, 0)
    before[...] = jnp.zeros_like(before)
    lax.fori_loop(0, planes - 1, source, 0)
    here = d_all[planes - 1]
    b_x[planes - 1] = jnp.zeros_like(here)
    s_part[planes - 1] = jnp.where(here > 0, before[...] + rest(planes - 1, here), 0.0)


def image(here, after, before, beta_x, beta_y, beta_z):
    flux_x = beta_x * (after - here)
    out = before - flux_x
    flux = beta_y * (next_row(here) - here)
    out = out + (prior_row(flux) - flux)
    flux = beta_z * (next_lane(here) - here)
    out = out + (prior_lane(flux) - flux)
    return jnp.where(beta_y > 0, out, 0.0), flux_x


def products(acc, here, out, beta_y, beta_z):
    own = slice(8, here.shape[0] - 8)
    jump = (next_row(out) - out)[own]
    here, out = here[own], out[own]
    jump_z = next_lane(out) - out
    acc[3] += fold(beta_y[own] * jump * jump + beta_z[own] * jump_z * jump_z)
    acc[0] += fold(here * here)
    acc[1] += fold(here * out)
    acc[2] += fold(out * out)


def jumps(acc, out, prior, beta_x):
    rows = prior.shape[0] - 8
    jump = out[8 : rows + 8] - prior[:rows]
    acc[3] += fold(beta_x[8 : rows + 8] * jump * jump)


def inner_kernel(s_part, b_x, b_y, b_z, s_far, q_far, ends, acc, q_out, before, sems):
    planes, rows = s_part.shape[0], s_part.shape[1]
    first, last = 2, planes - 3

    def leaving(x):
        return (
            pltpu.make_async_copy(s_part.at[x, pl.ds(8, rows - 8)], s_far.at[x], sems.at[0, x]),
            pltpu.make_async_copy(q_out.at[x], q_far.at[x], sems.at[1, x]),
        )

    def plane(x):
        here = s_part[x]
        out, flux = image(here, s_part[x + 1], before[...], b_x[x], b_y[x], b_z[x])
        before[...] = flux
        q_out[x] = out[8:]
        for copy in leaving(x):
            copy.start()
        products(acc, here, out, b_y[x], b_z[x])
        return out

    def inside(x, carry):
        jumps(acc, plane(x), q_out[x - 1], b_x[x - 1])
        return carry

    acc[...] = jnp.zeros_like(acc)
    before[...] = b_x[first - 1] * (s_part[first] - s_part[first - 1])
    plane(first)
    lax.fori_loop(first + 1, last + 1, inside, 0)
    ends[0] = q_out[first]
    ends[1] = q_out[last]
    for x in range(first, last + 1):
        for copy in leaving(x):
            copy.wait()


def moments_kernel(
    below_x, above_x, own_up, own_down, s_part, b_x, b_y, b_z, ends, inner, s_in, q_in,
    s_far, q_far, sums, s_out, q_out, acc, sems,
):
    planes = s_part.shape[0]
    last = planes - 1
    copies = []

    def leave(x, here, out):
        at = len(copies) // 2
        s_out[at] = here[8:]
        q_out[at] = out[8:]
        for kind, (source, to) in enumerate(((s_out, s_far), (q_out, q_far))):
            copies.append(pltpu.make_async_copy(source.at[at], to.at[x], sems.at[kind, at]))
            copies[-1].start()

    acc[...] = inner[...]
    beta = weight(below_x[0], own_down[0])
    flux = beta * below_x[1]
    here = s_part[0] + flux
    before = beta * (here - (below_x[2] - flux))
    out, before = image(here, s_part[1], before, b_x[0], b_y[0], b_z[0])
    products(acc, here, out, b_y[0], b_z[0])
    leave(0, here, out)
    here = s_part[1]
    out, before = image(here, s_part[2], before, b_x[1], b_y[1], b_z[1])
    products(acc, here, out, b_y[1], b_z[1])
    jumps(acc, out, q_out[0], b_x[0])
    leave(1, here, out)
    jump = ends[0, : s_part.shape[1] - 16, :] - q_out[1, : s_part.shape[1] - 16, :]
    acc[3] += fold(b_x[1, 8 : s_part.shape[1] - 8, :] * jump * jump)

    b_final = weight(own_up[0], above_x[0])
    flux = b_final * own_up[1]
    final = s_part[last] - flux
    s_after = jnp.where(above_x[0] > 0, above_x[2] + flux, 0.0)
    here = s_part[last - 1]
    before = b_x[last - 2] * (here - s_part[last - 2])
    out, before = image(here, final, before, b_x[last - 1], b_y[last - 1], b_z[last - 1])
    products(acc, here, out, b_y[last - 1], b_z[last - 1])
    jumps(acc, out, ends[1], b_x[last - 2])
    leave(last - 1, here, out)
    out, before = image(final, s_after, before, b_final, b_y[last], b_z[last])
    products(acc, final, out, b_y[last], b_z[last])
    jumps(acc, out, q_out[2], b_x[last - 1])
    leave(last, final, out)
    after = above_x[0]
    betas = weight(after, above_x[1]), weight(after, next_row(after)), weight(after, next_lane(after))
    out, _ = image(s_after, above_x[3], before, *betas)
    jumps(acc, out, q_out[3], b_final)
    leave(planes, s_after, out)
    at = lax.broadcasted_iota(jnp.int32, (1, 128), 1)
    row = jnp.zeros((1, 128), F32)
    for k in range(4):
        value = jnp.sum(jnp.sum(acc[k], 0, keepdims=True), 1, keepdims=True)
        row = row + jnp.where(at == k, value, 0.0)
    sums[...] = jnp.broadcast_to(row, sums.shape)
    for copy in copies:
        copy.wait()


def spreading(columns):
    at_column = lax.broadcasted_iota(jnp.int32, (64, columns), 1)
    return (at_column // 8 % 64 == lax.broadcasted_iota(jnp.int32, (64, columns), 0)).astype(F32)


def closure_kernel(
    sums, cot, s, q, s_next, q_next, feats, w_inner, w_outer,
    grad, grads, w_in, scale, velocity, hid, slope, vel, prod, acc_o, acc_t,
):
    step, planes = pl.program_id(0), cot.shape[1]
    rows, width = cot.shape[2], cot.shape[3]
    count = feats.shape[0]

    @pl.when(step == 0)
    def _():
        all_sums = jnp.sum(sums[...], 0, keepdims=True)
        at_lane = lax.broadcasted_iota(jnp.int32, (1, 128), 1)
        m0, m1, m2, m3 = (
            jnp.sum(jnp.where(at_lane == k, all_sums, 0.0), 1, keepdims=True) for k in range(4)
        )
        alpha0 = m0 / m1
        rr1 = jnp.maximum(alpha0 * alpha0 * m2 - m0, 0.0)
        beta = rr1 / m0
        more = 1.0 + beta
        alpha1 = rr1 / (more * more * m1 - 2.0 * more * alpha0 * m2 + alpha0 * alpha0 * m3)
        scale[0] = jnp.broadcast_to(alpha0 + alpha1 * more, scale.shape[1:])
        scale[1] = jnp.broadcast_to(-alpha1 * alpha0, scale.shape[1:])
        acc_o[...] = jnp.zeros_like(acc_o)
        acc_t[...] = jnp.zeros_like(acc_t)
        at_row, at_column = (lax.broadcasted_iota(jnp.int32, w_in.shape, k) for k in range(2))
        pick = lax.broadcasted_iota(jnp.int32, (w_in.shape[0], count), 0) // 16
        pick = (pick == lax.broadcasted_iota(jnp.int32, pick.shape, 1)).astype(BF16)
        tall = lax.dot_general(pick, w_inner[...], LAST, preferred_element_type=F32).astype(BF16)
        spread = jnp.dot(tall, spreading(w_in.shape[1]).astype(BF16), preferred_element_type=F32)
        same = at_row % 16 == at_column // (w_in.shape[1] // 2) * 8 + at_column % 8
        w_in[...] = jnp.where(same, spread, 0.0).astype(BF16)

    on_s, on_q = scale[0][:1], scale[1][:1]
    last = step == pl.num_programs(0) - 1
    beyond = on_s * s[0] + on_q * q[0]
    for x in range(planes):
        wide = beyond
        if x + 1 < planes:
            beyond = on_s * s[x + 1] + on_q * q[x + 1]
        else:
            beyond = on_s * s_next[0] + on_q * q_next[0]
        here = wide[:rows]
        for a, after in enumerate((beyond[:rows], next_row(wide)[:rows], next_lane(here))):
            value = cot[a, x] - (after - here)
            grad[a, x] = value
            velocity[a, x] = value.astype(BF16).astype(F32)

    half = w_in.shape[1] // 2
    per_plane, wide_tile = rows // 16, 256
    blocks = planes * per_plane

    def place_of(block):
        x, at = divmod(block, per_plane)
        return x, slice(at * 16, at * 16 + 16)

    def place(block, tile):
        part, column = divmod(tile * wide_tile, half)
        cells = (block * 2 + part) * width
        return slice(cells, cells + width), slice(column, column + wide_tile)

    def first_layer(block, tile):
        x, at = place_of(block)
        inner = feats[:, x, at, :].reshape(count * 16, width)
        weights = w_in[:, tile * wide_tile : (tile + 1) * wide_tile]
        pre = lax.dot_general(inner, weights, FIRST, preferred_element_type=F32)
        hidden = jnp.tanh(pre)
        to = place(block, tile)
        hid[to] = hidden.astype(BF16)
        slope[to] = (1.0 - hidden * hidden).astype(BF16)

    def outer(block, tile):
        cells, columns = place(block, tile)
        acc_o[:, columns] += jnp.dot(vel[:, cells], hid[cells, columns], preferred_element_type=F32)

    for block in range(blocks):
        x, at = place_of(block)
        broad = [feats[c, x, at, :].astype(F32) for c in range(count)]
        for part in range(2):
            to = slice((block * 2 + part) * width, (block * 2 + part + 1) * width)
            low = at.start + part * 8
            vs = [velocity[a, x, low : low + 8, :] for a in range(3)]
            vel[:, to] = jnp.concatenate(vs + [jnp.zeros_like(vs[0])], 0).astype(BF16)
            fs = [f[part * 8 : part * 8 + 8] for f in broad]
            prod[:, to] = jnp.concatenate([v * f for v in vs for f in fs], 0).astype(BF16)
    tiles = w_in.shape[1] // wide_tile
    late = 1
    for block in range(blocks + late):
        for tile in range(tiles):
            if block < blocks:
                first_layer(block, tile)
            if block >= late:
                outer(block - late, tile)
    acc_t[...] += jnp.dot(prod[...], slope[...], preferred_element_type=F32)

    @pl.when(last)
    def _():
        def own(value):
            at_row = lax.broadcasted_iota(jnp.int32, value.shape, 0) % 8
            at_col = lax.broadcasted_iota(jnp.int32, value.shape, 1) % 8
            kept = jnp.where(at_row == at_col, value, 0.0)
            return jnp.sum(kept.reshape(-1, 8, value.shape[1]), 1)

        outermost = own(acc_o[...])
        terms = own(acc_t[...])
        w_out = jnp.dot(w_outer[...], spreading(half).astype(BF16), preferred_element_type=F32)
        inner = sum(
            w_out[a : a + 1] * terms[a * count : (a + 1) * count] for a in range(3)
        )
        both = jnp.concatenate([inner, outermost[:3], jnp.zeros((5, half), F32)], 0)
        hidden_at = lax.broadcasted_iota(jnp.int32, (half, 64), 0) // 8
        column = lax.broadcasted_iota(jnp.int32, (half, 64), 1)
        pick = (hidden_at == column).astype(F32)
        sums16 = jnp.dot(both, pick, precision=lax.Precision.HIGHEST, preferred_element_type=F32)
        value = [sums16[k : k + 1] for k in (0, 4, 1, 5, 2, 6, 3, 7, 8, 10, 9, 11)]
        grads[...] = jnp.broadcast_to(jnp.concatenate(value, 1)[None], grads.shape)


def whole(shape):
    return pl.BlockSpec(shape, lambda i: (0,) * len(shape))


def shape(*dims):
    return jax.ShapeDtypeStruct(dims, F32)


def held(*dims):
    return pltpu.VMEM(dims, F32)


def keep(value):
    return pltpu.with_memory_space_constraint(value, pltpu.VMEM)


def away(value):
    return pltpu.with_memory_space_constraint(value, pltpu.HBM)


def params(mebibytes=24):
    return pltpu.CompilerParams(vmem_limit_bytes=mebibytes * 2**20)


def body(density, cotangent, features, w_inner, w_outer):
    nx, ny, nz = density.shape
    count, hidden = features.shape[0], w_inner.shape[0]
    devices = lax.axis_size("gx") * lax.axis_size("gy")
    cells = float(density.size * devices)
    lines = ny // 8 - 1
    near = pl.BlockSpec(memory_space=pltpu.VMEM)
    around = (ny + 16, nz)
    to_up, to_down = pl.pallas_call(
        pack_kernel,
        grid=(1,),
        in_specs=[
            pl.BlockSpec((nx, 8, nz), lambda i: (0, 0, 0)),
            pl.BlockSpec((nx, 8, nz), lambda i: (0, lines, 0)),
            pl.BlockSpec((3, nx, 8, nz), lambda i: (0, 0, 0, 0)),
            pl.BlockSpec((3, nx, 8, nz), lambda i: (0, 0, lines, 0)),
        ],
        out_specs=[whole((starts(plan)[1] * nx, nz)) for plan in (LOWER_Y, UPPER_Y)],
        out_shape=[shape(starts(plan)[1] * nx, nz) for plan in (LOWER_Y, UPPER_Y)],
        compiler_params=params(),
    )(*map(away, (density, density, cotangent, cotangent)))
    below_y, above_y = neighbours(to_up, 0, 1), neighbours(to_down, 0, -1)
    to_up, to_down = pl.pallas_call(
        edge_kernel,
        in_specs=[near] * 4,
        out_shape=[held(3, *around), held(4, *around)],
        compiler_params=params(12),
    )(*map(keep, (density, cotangent, below_y, above_y)))
    below_x, above_x = neighbours(to_up, 1, 0), neighbours(to_down, -1, 0)

    extended = (nx + 1, ny + 8, nz)
    whole_planes = (nx,) + around
    fields = pl.pallas_call(
        source_kernel,
        in_specs=[near] * 4,
        out_shape=[held(*whole_planes)] * 4,
        scratch_shapes=[pltpu.VMEM(whole_planes, F32), pltpu.VMEM(around, F32)],
        compiler_params=params(12),
    )(*map(keep, (density, cotangent, below_y, above_y)))
    far = pl.BlockSpec(memory_space=pltpu.HBM)
    s, q, ends, inner = pl.pallas_call(
        inner_kernel,
        in_specs=[near] * 4,
        out_specs=[far] * 2 + [near] * 2,
        out_shape=[pltpu.HBM(extended, F32)] * 2 + [held(2, *extended[1:]), held(4, 8, nz)],
        scratch_shapes=[
            pltpu.VMEM(extended, F32),
            pltpu.VMEM(around, F32),
            pltpu.SemaphoreType.DMA((2, nx)),
        ],
        compiler_params=params(12),
    )(*fields)
    s, q, sums = pl.pallas_call(
        moments_kernel,
        in_specs=[near] * 10 + [far] * 2,
        out_specs=[far] * 2 + [near],
        out_shape=[pltpu.HBM(extended, F32)] * 2 + [held(devices, 128)],
        input_output_aliases={10: 0, 11: 1},
        scratch_shapes=[pltpu.VMEM((5,) + extended[1:], F32)] * 2
        + [pltpu.VMEM((4, 8, nz), F32), pltpu.SemaphoreType.DMA((2, 5))],
        compiler_params=params(16),
    )(*map(keep, (below_x, above_x, to_up, to_down, *fields, ends, inner)), s, q)
    sums = collect(sums)

    half = hidden * 8
    step = 2
    long = step * ny // 8 * nz
    planes = pl.BlockSpec((3, step, ny, nz), lambda i: (0, i, 0, 0))
    here = pl.BlockSpec((step, ny + 8, nz), lambda i: (i, 0, 0))
    after = pl.BlockSpec((1, ny + 8, nz), lambda i: (step * i + step, 0, 0))
    grad, grads = pl.pallas_call(
        closure_kernel,
        grid=(nx // step,),
        in_specs=[
            whole((devices, 128)), planes, here, here, after, after,
            pl.BlockSpec((count, step, ny, nz), lambda i: (0, i, 0, 0)), whole(w_inner.shape), whole(w_outer.shape),
        ],
        out_specs=[planes, whole((devices, 1, 768))],
        out_shape=[shape(3, nx, ny, nz), shape(devices, 1, 768)],
        scratch_shapes=[
            pltpu.VMEM((count * 16, 2 * half), BF16),
            pltpu.VMEM((2, 8, nz), F32),
            pltpu.VMEM((3, step, ny, nz), F32),
            pltpu.VMEM((long, half), BF16),
            pltpu.VMEM((long, half), BF16),
            pltpu.VMEM((32, long), BF16),
            pltpu.VMEM((24 * count, long), BF16),
            pltpu.VMEM((32, half), F32),
            pltpu.VMEM((24 * count, half), F32),
        ],
        compiler_params=params(48),
    )(keep(sums), *map(away, (cotangent, s, q, s, q, features)), w_inner, w_outer)
    grads = jnp.sum(collect(grads), 0).reshape(6, 128) / cells
    low, high = grads[:, :hidden], grads[:, hidden:]
    return grad, jnp.concatenate([low[:4], high[:4]]).T, jnp.concatenate([low[4:], high[4:5]])


def solution(mesh):
    in_specs = (P("gx", "gy", None), P(None, "gx", "gy", None), P(None, "gx", "gy", None), P(), P())
    out_specs = (P(None, "gx", "gy", None), P(), P())
    return jax.shard_map(body, mesh=mesh, in_specs=in_specs, out_specs=out_specs, check_vma=False)
```

```python
import jax
import jax.numpy as jnp
from jax import lax
from jax.experimental import pallas as pl
from jax.experimental.pallas import tpu as pltpu
from jax.sharding import PartitionSpec as P

F32 = jnp.float32
BF16 = jnp.bfloat16
FIRST = (((0,), (0,)), ((), ()))
LAST = (((1,), (1,)), ((), ()))


def collect(copies):
    return lax.all_to_all(copies, ("gx", "gy"), 0, 0)


def neighbours(value, by_x, by_y):
    nx, ny = lax.axis_size("gx"), lax.axis_size("gy")
    pairs = [
        (i * ny + j, (i + by_x) * ny + j + by_y)
        for i in range(nx)
        for j in range(ny)
        if 0 <= i + by_x < nx and 0 <= j + by_y < ny
    ]
    return lax.ppermute(value, ("gx", "gy"), pairs)


def next_lane(plane):
    size = plane.shape[1]
    at = lax.broadcasted_iota(jnp.int32, plane.shape, 1)
    return jnp.where(at == size - 1, 0.0, pltpu.roll(plane, size - 1, 1))


def prior_lane(plane):
    at = lax.broadcasted_iota(jnp.int32, plane.shape, 1)
    return jnp.where(at == 0, 0.0, pltpu.roll(plane, 1, 1))


def next_row(plane):
    return pltpu.roll(plane, plane.shape[0] - 1, 0)


def prior_row(plane):
    return pltpu.roll(plane, 1, 0)


def fold(plane):
    return jnp.sum(plane.reshape(-1, 8, plane.shape[1]), 0)


LOWER_Y = ((0, 2), (1, 1), (2, 2), (3, 1))
UPPER_Y = ((0, 3), (1, 2), (2, 2), (3, 2))


def starts(plan):
    places, at = [], 0
    for _, width in plan:
        places.append(at)
        at += width
    return places, at


def pack_kernel(d_first, d_last, c_first, c_last, up, down):
    planes = d_first.shape[0]

    def line(field, x, y):
        if field == 0:
            block = d_first if y >= 0 else d_last
            return block[x, y % 8 : y % 8 + 1, :]
        block = c_first if y >= 0 else c_last
        return block[field - 1, x, y % 8 : y % 8 + 1, :]

    for plan, to, low in ((LOWER_Y, up, False), (UPPER_Y, down, True)):
        at = 0
        for field, width in plan:
            for y in range(width):
                for x in range(planes):
                    to[at : at + 1, :] = line(field, x, y if low else y - width)
                    at += 1


def sides(below_y, above_y, planes, field, x):
    low, high, width = LOWER_Y[field][1], UPPER_Y[field][1], below_y.shape[1]
    low_at, high_at = starts(LOWER_Y)[0][field], starts(UPPER_Y)[0][field]
    below = [below_y[pl.ds((low_at + k) * planes + x, 1), :] for k in range(low)]
    above = [above_y[pl.ds((high_at + k) * planes + x, 1), :] for k in range(high)]
    below = jnp.concatenate([jnp.zeros((8 - low, width), F32)] + below, 0)
    return below, jnp.concatenate(above + [jnp.zeros((8 - high, width), F32)], 0)


def weight(value, after):
    return jnp.where(value > 0, 2.0 / (value + after), 0.0)


def across(here, beta_y, beta_z, cot_y, cot_z):
    flux_y, flux_z = beta_y * cot_y, beta_z * cot_z
    return prior_row(flux_y) - flux_y + (prior_lane(flux_z) - flux_z)


def edge_kernel(dens, cot, below_y, above_y, up, down):
    planes = dens.shape[0]

    def plane(field, x):
        low, high = sides(below_y, above_y, planes, field, x)
        return jnp.concatenate([low, dens[x] if field == 0 else cot[field - 1, x], high], 0)

    def part(x):
        here = plane(0, x)
        return across(here, weight(here, next_row(here)), weight(here, next_lane(here)), plane(2, x), plane(3, x))

    last = planes - 1
    here, before = plane(0, last), plane(0, last - 1)
    up[0] = here
    up[1] = plane(1, last)
    up[2] = jnp.where(here > 0, weight(before, here) * plane(1, last - 1) + part(last), 0.0)
    here, after = plane(0, 0), plane(0, 1)
    down[0] = here
    down[1] = after
    flux = weight(here, after) * plane(1, 0)
    down[2] = jnp.where(here > 0, part(0) - flux, 0.0)
    down[3] = jnp.where(after > 0, flux - weight(after, plane(0, 2)) * plane(1, 1) + part(1), 0.0)


def source_kernel(
    dens, cot, below_y, above_y, s_part, b_x, b_y, b_z, d_all, before
):
    planes, rows, width = dens.shape

    def fill(x, carry):
        low, high = sides(below_y, above_y, planes, 0, x)
        d_all[x, 0:8, :] = low
        d_all[x, 8 : rows + 8, :] = dens[x]
        d_all[x, rows + 8 : rows + 16, :] = high
        return carry

    def field(index, x):
        low, high = sides(below_y, above_y, planes, index, x)
        return jnp.concatenate([low, cot[index - 1, x], high], 0)

    def rest(x, here):
        b_y[x] = weight(here, next_row(here))
        b_z[x] = weight(here, next_lane(here))
        return across(here, b_y[x], b_z[x], field(2, x), field(3, x))

    def source(x, carry):
        here = d_all[x]
        b_x[x] = weight(here, d_all[x + 1])
        flux = b_x[x] * field(1, x)
        out = before[...] - flux + rest(x, here)
        before[...] = flux
        s_part[x] = jnp.where(here > 0, out, 0.0)
        return carry

    lax.fori_loop(0, planes, fill, 0)
    before[...] = jnp.zeros_like(before)
    lax.fori_loop(0, planes - 1, source, 0)
    here = d_all[planes - 1]
    b_x[planes - 1] = jnp.zeros_like(here)
    s_part[planes - 1] = jnp.where(here > 0, before[...] + rest(planes - 1, here), 0.0)


def image(here, after, before, beta_x, beta_y, beta_z):
    flux_x = beta_x * (after - here)
    out = before - flux_x
    flux = beta_y * (next_row(here) - here)
    out = out + (prior_row(flux) - flux)
    flux = beta_z * (next_lane(here) - here)
    out = out + (prior_lane(flux) - flux)
    return jnp.where(beta_y > 0, out, 0.0), flux_x


def products(acc, here, out, beta_y, beta_z):
    own = slice(8, here.shape[0] - 8)
    jump = (next_row(out) - out)[own]
    here, out = here[own], out[own]
    jump_z = next_lane(out) - out
    acc[3] += fold(beta_y[own] * jump * jump + beta_z[own] * jump_z * jump_z)
    acc[0] += fold(here * here)
    acc[1] += fold(here * out)
    acc[2] += fold(out * out)


def jumps(acc, out, prior, beta_x):
    rows = prior.shape[0] - 8
    jump = out[8 : rows + 8] - prior[:rows]
    acc[3] += fold(beta_x[8 : rows + 8] * jump * jump)


def inner_kernel(s_part, b_x, b_y, b_z, s_far, q_far, ends, acc, q_out, before, sems):
    planes, rows = s_part.shape[0], s_part.shape[1]
    first, last = 2, planes - 3

    def leaving(x):
        return (
            pltpu.make_async_copy(s_part.at[x, pl.ds(8, rows - 8)], s_far.at[x], sems.at[0, x]),
            pltpu.make_async_copy(q_out.at[x], q_far.at[x], sems.at[1, x]),
        )

    def plane(x):
        here = s_part[x]
        out, flux = image(here, s_part[x + 1], before[...], b_x[x], b_y[x], b_z[x])
        before[...] = flux
        q_out[x] = out[8:]
        for copy in leaving(x):
            copy.start()
        products(acc, here, out, b_y[x], b_z[x])
        return out

    def inside(x, carry):
        jumps(acc, plane(x), q_out[x - 1], b_x[x - 1])
        return carry

    acc[...] = jnp.zeros_like(acc)
    before[...] = b_x[first - 1] * (s_part[first] - s_part[first - 1])
    plane(first)
    lax.fori_loop(first + 1, last + 1, inside, 0)
    ends[0] = q_out[first]
    ends[1] = q_out[last]
    for x in range(first, last + 1):
        for copy in leaving(x):
            copy.wait()


def moments_kernel(
    below_x, above_x, own_up, own_down, s_part, b_x, b_y, b_z, ends, inner, s_in, q_in,
    s_far, q_far, sums, s_out, q_out, acc, sems,
):
    planes = s_part.shape[0]
    last = planes - 1
    copies = []

    def leave(x, here, out):
        at = len(copies) // 2
        s_out[at] = here[8:]
        q_out[at] = out[8:]
        for kind, (source, to) in enumerate(((s_out, s_far), (q_out, q_far))):
            copies.append(pltpu.make_async_copy(source.at[at], to.at[x], sems.at[kind, at]))
            copies[-1].start()

    acc[...] = inner[...]
    beta = weight(below_x[0], own_down[0])
    flux = beta * below_x[1]
    here = s_part[0] + flux
    before = beta * (here - (below_x[2] - flux))
    out, before = image(here, s_part[1], before, b_x[0], b_y[0], b_z[0])
    products(acc, here, out, b_y[0], b_z[0])
    leave(0, here, out)
    here = s_part[1]
    out, before = image(here, s_part[2], before, b_x[1], b_y[1], b_z[1])
    products(acc, here, out, b_y[1], b_z[1])
    jumps(acc, out, q_out[0], b_x[0])
    leave(1, here, out)
    jump = ends[0, : s_part.shape[1] - 16, :] - q_out[1, : s_part.shape[1] - 16, :]
    acc[3] += fold(b_x[1, 8 : s_part.shape[1] - 8, :] * jump * jump)

    b_final = weight(own_up[0], above_x[0])
    flux = b_final * own_up[1]
    final = s_part[last] - flux
    s_after = jnp.where(above_x[0] > 0, above_x[2] + flux, 0.0)
    here = s_part[last - 1]
    before = b_x[last - 2] * (here - s_part[last - 2])
    out, before = image(here, final, before, b_x[last - 1], b_y[last - 1], b_z[last - 1])
    products(acc, here, out, b_y[last - 1], b_z[last - 1])
    jumps(acc, out, ends[1], b_x[last - 2])
    leave(last - 1, here, out)
    out, before = image(final, s_after, before, b_final, b_y[last], b_z[last])
    products(acc, final, out, b_y[last], b_z[last])
    jumps(acc, out, q_out[2], b_x[last - 1])
    leave(last, final, out)
    after = above_x[0]
    betas = weight(after, above_x[1]), weight(after, next_row(after)), weight(after, next_lane(after))
    out, _ = image(s_after, above_x[3], before, *betas)
    jumps(acc, out, q_out[3], b_final)
    leave(planes, s_after, out)
    at = lax.broadcasted_iota(jnp.int32, (1, 128), 1)
    row = jnp.zeros((1, 128), F32)
    for k in range(4):
        value = jnp.sum(jnp.sum(acc[k], 0, keepdims=True), 1, keepdims=True)
        row = row + jnp.where(at == k, value, 0.0)
    sums[...] = jnp.broadcast_to(row, sums.shape)
    for copy in copies:
        copy.wait()


def spreading(columns):
    at_column = lax.broadcasted_iota(jnp.int32, (64, columns), 1)
    return (at_column // 8 % 64 == lax.broadcasted_iota(jnp.int32, (64, columns), 0)).astype(F32)


def closure_kernel(
    sums, cot, s, q, s_next, q_next, feats, w_inner, w_outer,
    grad, grads, w_in, scale, velocity, hid, slope, vel, prod, acc_o, acc_t,
):
    step, planes = pl.program_id(0), cot.shape[1]
    rows, width = cot.shape[2], cot.shape[3]
    count = feats.shape[0]

    @pl.when(step == 0)
    def _():
        all_sums = jnp.sum(sums[...], 0, keepdims=True)
        at_lane = lax.broadcasted_iota(jnp.int32, (1, 128), 1)
        m0, m1, m2, m3 = (
            jnp.sum(jnp.where(at_lane == k, all_sums, 0.0), 1, keepdims=True) for k in range(4)
        )
        alpha0 = m0 / m1
        rr1 = jnp.maximum(alpha0 * alpha0 * m2 - m0, 0.0)
        beta = rr1 / m0
        more = 1.0 + beta
        alpha1 = rr1 / (more * more * m1 - 2.0 * more * alpha0 * m2 + alpha0 * alpha0 * m3)
        scale[0] = jnp.broadcast_to(alpha0 + alpha1 * more, scale.shape[1:])
        scale[1] = jnp.broadcast_to(-alpha1 * alpha0, scale.shape[1:])
        acc_o[...] = jnp.zeros_like(acc_o)
        acc_t[...] = jnp.zeros_like(acc_t)
        at_row, at_column = (lax.broadcasted_iota(jnp.int32, w_in.shape, k) for k in range(2))
        pick = lax.broadcasted_iota(jnp.int32, (w_in.shape[0], count), 0) // 16
        pick = (pick == lax.broadcasted_iota(jnp.int32, pick.shape, 1)).astype(BF16)
        tall = lax.dot_general(pick, w_inner[...], LAST, preferred_element_type=F32).astype(BF16)
        spread = jnp.dot(tall, spreading(w_in.shape[1]).astype(BF16), preferred_element_type=F32)
        same = at_row % 16 == at_column // (w_in.shape[1] // 2) * 8 + at_column % 8
        w_in[...] = jnp.where(same, spread, 0.0).astype(BF16)

    on_s, on_q = scale[0][:1], scale[1][:1]
    last = step == pl.num_programs(0) - 1
    beyond = on_s * s[0] + on_q * q[0]
    for x in range(planes):
        wide = beyond
        if x + 1 < planes:
            beyond = on_s * s[x + 1] + on_q * q[x + 1]
        else:
            beyond = on_s * s_next[0] + on_q * q_next[0]
        here = wide[:rows]
        for a, after in enumerate((beyond[:rows], next_row(wide)[:rows], next_lane(here))):
            value = cot[a, x] - (after - here)
            grad[a, x] = value
            velocity[a, x] = value.astype(BF16).astype(F32)

    half = w_in.shape[1] // 2
    per_plane, wide_tile = rows // 16, 256
    blocks = planes * per_plane

    def place_of(block):
        x, at = divmod(block, per_plane)
        return x, slice(at * 16, at * 16 + 16)

    def place(block, tile):
        part, column = divmod(tile * wide_tile, half)
        cells = (block * 2 + part) * width
        return slice(cells, cells + width), slice(column, column + wide_tile)

    def first_layer(block, tile):
        x, at = place_of(block)
        inner = feats[:, x, at, :].reshape(count * 16, width)
        weights = w_in[:, tile * wide_tile : (tile + 1) * wide_tile]
        pre = lax.dot_general(inner, weights, FIRST, preferred_element_type=F32)
        hidden = jnp.tanh(pre)
        to = place(block, tile)
        hid[to] = hidden.astype(BF16)
        slope[to] = (1.0 - hidden * hidden).astype(BF16)

    def outer(block, tile):
        cells, columns = place(block, tile)
        acc_o[:, columns] += jnp.dot(vel[:, cells], hid[cells, columns], preferred_element_type=F32)

    def right(block):
        x, at = place_of(block)
        broad = [feats[c, x, at, :].astype(F32) for c in range(count)]
        for part in range(2):
            to = slice((block * 2 + part) * width, (block * 2 + part + 1) * width)
            low = at.start + part * 8
            vs = [velocity[a, x, low : low + 8, :] for a in range(3)]
            vel[:, to] = jnp.concatenate(vs + [jnp.zeros_like(vs[0])], 0).astype(BF16)
            fs = [f[part * 8 : part * 8 + 8] for f in broad]
            prod[:, to] = jnp.concatenate([v * f for v in vs for f in fs], 0).astype(BF16)

    tiles = w_in.shape[1] // wide_tile
    late = 1
    for block in range(blocks + late):
        for tile in range(tiles):
            if block < blocks:
                first_layer(block, tile)
                if tile == 1:
                    right(block)
            if block >= late:
                outer(block - late, tile)
    acc_t[...] += jnp.dot(prod[...], slope[...], preferred_element_type=F32)

    @pl.when(last)
    def _():
        def own(value):
            at_row = lax.broadcasted_iota(jnp.int32, value.shape, 0) % 8
            at_col = lax.broadcasted_iota(jnp.int32, value.shape, 1) % 8
            kept = jnp.where(at_row == at_col, value, 0.0)
            return jnp.sum(kept.reshape(-1, 8, value.shape[1]), 1)

        outermost = own(acc_o[...])
        terms = own(acc_t[...])
        w_out = jnp.dot(w_outer[...], spreading(half).astype(BF16), preferred_element_type=F32)
        inner = sum(
            w_out[a : a + 1] * terms[a * count : (a + 1) * count] for a in range(3)
        )
        both = jnp.concatenate([inner, outermost[:3], jnp.zeros((5, half), F32)], 0)
        hidden_at = lax.broadcasted_iota(jnp.int32, (half, 64), 0) // 8
        column = lax.broadcasted_iota(jnp.int32, (half, 64), 1)
        pick = (hidden_at == column).astype(F32)
        sums16 = jnp.dot(both, pick, precision=lax.Precision.HIGHEST, preferred_element_type=F32)
        value = [sums16[k : k + 1] for k in (0, 4, 1, 5, 2, 6, 3, 7, 8, 10, 9, 11)]
        grads[...] = jnp.broadcast_to(jnp.concatenate(value, 1)[None], grads.shape)


def whole(shape):
    return pl.BlockSpec(shape, lambda i: (0,) * len(shape))


def shape(*dims):
    return jax.ShapeDtypeStruct(dims, F32)


def held(*dims):
    return pltpu.VMEM(dims, F32)


def keep(value):
    return pltpu.with_memory_space_constraint(value, pltpu.VMEM)


def away(value):
    return pltpu.with_memory_space_constraint(value, pltpu.HBM)


def params(mebibytes=24):
    return pltpu.CompilerParams(vmem_limit_bytes=mebibytes * 2**20)


def body(density, cotangent, features, w_inner, w_outer):
    nx, ny, nz = density.shape
    count, hidden = features.shape[0], w_inner.shape[0]
    devices = lax.axis_size("gx") * lax.axis_size("gy")
    cells = float(density.size * devices)
    lines = ny // 8 - 1
    near = pl.BlockSpec(memory_space=pltpu.VMEM)
    around = (ny + 16, nz)
    to_up, to_down = pl.pallas_call(
        pack_kernel,
        grid=(1,),
        in_specs=[
            pl.BlockSpec((nx, 8, nz), lambda i: (0, 0, 0)),
            pl.BlockSpec((nx, 8, nz), lambda i: (0, lines, 0)),
            pl.BlockSpec((3, nx, 8, nz), lambda i: (0, 0, 0, 0)),
            pl.BlockSpec((3, nx, 8, nz), lambda i: (0, 0, lines, 0)),
        ],
        out_specs=[whole((starts(plan)[1] * nx, nz)) for plan in (LOWER_Y, UPPER_Y)],
        out_shape=[shape(starts(plan)[1] * nx, nz) for plan in (LOWER_Y, UPPER_Y)],
        compiler_params=params(),
    )(*map(away, (density, density, cotangent, cotangent)))
    below_y, above_y = neighbours(to_up, 0, 1), neighbours(to_down, 0, -1)
    to_up, to_down = pl.pallas_call(
        edge_kernel,
        in_specs=[near] * 4,
        out_shape=[held(3, *around), held(4, *around)],
        compiler_params=params(12),
    )(*map(keep, (density, cotangent, below_y, above_y)))
    below_x, above_x = neighbours(to_up, 1, 0), neighbours(to_down, -1, 0)

    extended = (nx + 1, ny + 8, nz)
    whole_planes = (nx,) + around
    fields = pl.pallas_call(
        source_kernel,
        in_specs=[near] * 4,
        out_shape=[held(*whole_planes)] * 4,
        scratch_shapes=[pltpu.VMEM(whole_planes, F32), pltpu.VMEM(around, F32)],
        compiler_params=params(12),
    )(*map(keep, (density, cotangent, below_y, above_y)))
    far = pl.BlockSpec(memory_space=pltpu.HBM)
    s, q, ends, inner = pl.pallas_call(
        inner_kernel,
        in_specs=[near] * 4,
        out_specs=[far] * 2 + [near] * 2,
        out_shape=[pltpu.HBM(extended, F32)] * 2 + [held(2, *extended[1:]), held(4, 8, nz)],
        scratch_shapes=[
            pltpu.VMEM(extended, F32),
            pltpu.VMEM(around, F32),
            pltpu.SemaphoreType.DMA((2, nx)),
        ],
        compiler_params=params(12),
    )(*fields)
    s, q, sums = pl.pallas_call(
        moments_kernel,
        in_specs=[near] * 10 + [far] * 2,
        out_specs=[far] * 2 + [near],
        out_shape=[pltpu.HBM(extended, F32)] * 2 + [held(devices, 128)],
        input_output_aliases={10: 0, 11: 1},
        scratch_shapes=[pltpu.VMEM((5,) + extended[1:], F32)] * 2
        + [pltpu.VMEM((4, 8, nz), F32), pltpu.SemaphoreType.DMA((2, 5))],
        compiler_params=params(16),
    )(*map(keep, (below_x, above_x, to_up, to_down, *fields, ends, inner)), s, q)
    sums = collect(sums)

    half = hidden * 8
    step = 4
    long = step * ny // 8 * nz
    planes = pl.BlockSpec((3, step, ny, nz), lambda i: (0, i, 0, 0))
    here = pl.BlockSpec((step, ny + 8, nz), lambda i: (i, 0, 0))
    after = pl.BlockSpec((1, ny + 8, nz), lambda i: (step * i + step, 0, 0))
    grad, grads = pl.pallas_call(
        closure_kernel,
        grid=(nx // step,),
        in_specs=[
            whole((devices, 128)), planes, here, here, after, after,
            pl.BlockSpec((count, step, ny, nz), lambda i: (0, i, 0, 0)), whole(w_inner.shape), whole(w_outer.shape),
        ],
        out_specs=[planes, whole((devices, 1, 768))],
        out_shape=[shape(3, nx, ny, nz), shape(devices, 1, 768)],
        scratch_shapes=[
            pltpu.VMEM((count * 16, 2 * half), BF16),
            pltpu.VMEM((2, 8, nz), F32),
            pltpu.VMEM((3, step, ny, nz), F32),
            pltpu.VMEM((long, half), BF16),
            pltpu.VMEM((long, half), BF16),
            pltpu.VMEM((32, long), BF16),
            pltpu.VMEM((24 * count, long), BF16),
            pltpu.VMEM((32, half), F32),
            pltpu.VMEM((24 * count, half), F32),
        ],
        compiler_params=params(60),
    )(keep(sums), *map(away, (cotangent, s, q, s, q, features)), w_inner, w_outer)
    grads = jnp.sum(collect(grads), 0).reshape(6, 128) / cells
    low, high = grads[:, :hidden], grads[:, hidden:]
    return grad, jnp.concatenate([low[:4], high[:4]]).T, jnp.concatenate([low[4:], high[4:5]])


def solution(mesh):
    in_specs = (P("gx", "gy", None), P(None, "gx", "gy", None), P(None, "gx", "gy", None), P(), P())
    out_specs = (P(None, "gx", "gy", None), P(), P())
    return jax.shard_map(body, mesh=mesh, in_specs=in_specs, out_specs=out_specs, check_vma=False)
```
